128 devices in a mesh: row: 16 (over x_lo, z, core), col: 8 (over x_hi, y).
Axes of the slice: x: 4 (x_hi: 2, x_lo: 2; x = x_hi * 2 + x_lo), y: 4, z: 4, core: 2. Of those that a mesh axis runs over, the one named last changes fastest.
Arguments:
- pair: bfloat16 [512, 512, 128], P('row', 'col')
- valid_len: int32 [1], replicated, may hold values from 256 to 512
- tri_in: bfloat16 [128, 512], replicated, may hold values from -0.5 to 0.5
- tri_gate: bfloat16 [128, 128], replicated, may hold values from -0.5 to 0.5
- tri_out: bfloat16 [128, 128], replicated, may hold values from -0.5 to 0.5
- att_qkvg: bfloat16 [128, 512], replicated, may hold values from -0.5 to 0.5
- att_bias: bfloat16 [128, 4], replicated
- att_out: bfloat16 [128, 128], replicated, may hold values from -0.5 to 0.5
Outputs:
- updated: bfloat16 [512, 512, 128], P('row', 'col')
The draws below stay inside these ranges and needn't reach their ends.
All inputs are finite; a program needn't handle non-finite values.
Results may differ from the reference program's by a relative error of at most 0.012.
Values may be sent and summed in bfloat16 or wider, within the bound.
A program may use at most 128 MiB of HBM per device.

```python
import jax
import jax.numpy as jnp
from jax import lax

C = 128
HID = 128
HEADS = 4
DH = 32
N = 512


def draw_pair(key, part):
    key = jax.random.fold_in(key, 11)
    base = jnp.clip(jax.random.normal(key, (N, N, C), jnp.float32), -6.0, 6.0)
    return base.astype(jnp.bfloat16)


def draw_att_bias(key, part):
    key = jax.random.fold_in(key, 13)
    weight = jax.random.normal(key, (C, HEADS), jnp.float32) / jnp.sqrt(jnp.float32(C))
    return weight.astype(jnp.bfloat16)


def gaussian(stream_key, extent, spread, most, held_as=jnp.bfloat16):
    values = spread * jax.random.normal(stream_key, extent, jnp.float32)
    return jnp.clip(values, min=-most, max=most).astype(held_as)


def setup_inputs(seed: int = 0) -> dict:
    splits = jax.random.split(jax.random.key(seed), 9)
    return {
        "pair": draw_pair(jax.random.fold_in(splits[8], 71), 0),
        "valid_len": jax.random.randint(splits[1], (1,), N // 2, N + 1).astype(jnp.int32),
        "tri_in": gaussian(splits[2], (C, 4 * HID), C ** -0.5, 0.5),
        "tri_gate": gaussian(splits[3], (C, C), C ** -0.5, 0.5),
        "tri_out": gaussian(splits[4], (HID, C), HID ** -0.5, 0.5),
        "att_qkvg": gaussian(splits[5], (C, 4 * C), C ** -0.5, 0.5),
        "att_bias": draw_att_bias(jax.random.fold_in(splits[8], 71), 0),
        "att_out": gaussian(splits[7], (C, C), C ** -0.5, 0.5),
    }


def layer_norm(values):
    mean = lax.optimization_barrier(jnp.mean(values, axis=-1, keepdims=True))
    centred = values - mean
    var = lax.optimization_barrier(jnp.mean(centred * centred, axis=-1, keepdims=True))
    return centred * lax.rsqrt(var + 1e-05)

def reference(pair, valid_len, tri_in, tri_gate, tri_out, att_qkvg, att_bias, att_out):
    limit = valid_len[0]
    keep = jnp.arange(N) < limit
    pmask = (keep[:, None] & keep[None, :]).astype(jnp.float32)[..., None]
    pairf = pair.astype(jnp.float32)
    normed = layer_norm(pairf).astype(jnp.bfloat16)
    proj = jnp.dot(normed, tri_in, preferred_element_type=jnp.float32)
    left = (jax.nn.sigmoid(proj[..., :HID]) * proj[..., HID:2 * HID] * pmask).astype(jnp.bfloat16)
    right = (jax.nn.sigmoid(proj[..., 2 * HID:3 * HID]) * proj[..., 3 * HID:] * pmask).astype(jnp.bfloat16)
    tgate = jax.nn.sigmoid(jnp.dot(normed, tri_gate, preferred_element_type=jnp.float32))
    product = jnp.einsum('ikc,jkc->ijc', left.astype(jnp.float32), right.astype(jnp.float32), precision=lax.Precision.HIGHEST)
    prodnorm = layer_norm(product).astype(jnp.bfloat16)
    first = (pairf + tgate * jnp.dot(prodnorm, tri_out, preferred_element_type=jnp.float32)).astype(jnp.bfloat16)
    firstf = first.astype(jnp.float32)
    second_norm = layer_norm(firstf).astype(jnp.bfloat16)
    qkvg = jnp.dot(second_norm, att_qkvg, preferred_element_type=jnp.float32)
    query = qkvg[..., :C].astype(jnp.bfloat16)
    keys = qkvg[..., C:2 * C].astype(jnp.bfloat16)
    values = qkvg[..., 2 * C:3 * C].astype(jnp.bfloat16)
    agate = jax.nn.sigmoid(qkvg[..., 3 * C:])
    bias = jnp.dot(second_norm, att_bias, preferred_element_type=jnp.float32).astype(jnp.bfloat16)
    bias_heads = jnp.transpose(bias, (2, 0, 1)).astype(jnp.float32)
    key_bias = jnp.where(keep, 0.0, -1000000000.0).astype(jnp.float32)
    scale = DH ** (-0.5)

    def one_row(items):
        q_row, k_row, v_row = items
        qh = q_row.reshape(N, HEADS, DH).astype(jnp.float32)
        kh = k_row.reshape(N, HEADS, DH).astype(jnp.float32)
        vh = v_row.reshape(N, HEADS, DH).astype(jnp.float32)
        scores = jnp.einsum('jhd,khd->hjk', qh, kh) * scale + bias_heads + key_bias
        top = lax.optimization_barrier(jnp.max(scores, axis=-1, keepdims=True))
        expo = jnp.exp(scores - top)
        total = lax.optimization_barrier(jnp.sum(expo, axis=-1, keepdims=True))
        weights = expo.astype(jnp.bfloat16).astype(jnp.float32)
        out = jnp.einsum('hjk,khd->jhd', weights, vh) / jnp.transpose(total, (1, 0, 2))
        return out.reshape(N, C)
    att = lax.map(one_row, (query, keys, values))
    gated = (agate * att).astype(jnp.bfloat16)
    return (firstf + jnp.dot(gated, att_out, preferred_element_type=jnp.float32)).astype(jnp.bfloat16)
```

```python
import functools

import jax
import jax.numpy as jnp
from jax import lax
from jax.experimental import pallas as pl
from jax.experimental.pallas import tpu as pltpu
from jax.sharding import PartitionSpec as P

MESH = pl.DeviceIdType.MESH


def layer_norm(values, axis):
    mean = jnp.mean(values, axis=axis, keepdims=True)
    centred = values - mean
    var = jnp.mean(centred * centred, axis=axis, keepdims=True)
    return centred * lax.rsqrt(var + 1e-05)


def place(whole, n_col, index):
    if whole:
        return (index // n_col, lax.rem(index, n_col))
    return (lax.axis_index("row"), index)


def exchange_kernel(n, n_col, whole, same, src, dst, send_sem, recv_sem, own_sem):
    me = lax.axis_index("col")
    if whole:
        me = lax.axis_index("row") * n_col + me
    barrier = pltpu.get_barrier_semaphore()

    def greet(step, carry):
        target = lax.rem(me + step, n)
        pl.semaphore_signal(
            barrier, inc=1, device_id=place(whole, n_col, target), device_id_type=MESH
        )
        return carry

    lax.fori_loop(1, n, greet, 0)
    pl.semaphore_wait(barrier, n - 1)
    own = pltpu.make_async_copy(src if same else src.at[me], dst.at[me], own_sem)
    own.start()

    def send(step, carry):
        target = lax.rem(me + step, n)
        pltpu.make_async_remote_copy(
            src_ref=src if same else src.at[target],
            dst_ref=dst.at[me],
            send_sem=send_sem,
            recv_sem=recv_sem,
            device_id=place(whole, n_col, target),
            device_id_type=MESH,
        ).start()
        return carry

    lax.fori_loop(1, n, send, 0)
    own.wait()
    others = dst.at[pl.ds(0, n - 1)]
    pltpu.make_async_copy(others, others, send_sem).wait()
    pltpu.make_async_copy(others, others, recv_sem).wait()


def exchange(array, n, n_col, collective_id, whole=True, same=False):
    shape = (n,) + array.shape if same else array.shape
    return pl.pallas_call(
        functools.partial(exchange_kernel, n, n_col, whole, same),
        out_shape=jax.ShapeDtypeStruct(shape, array.dtype),
        in_specs=[pl.BlockSpec(memory_space=pltpu.VMEM)],
        out_specs=pl.BlockSpec(memory_space=pltpu.VMEM),
        scratch_shapes=[pltpu.SemaphoreType.DMA] * 3,
        compiler_params=pltpu.CompilerParams(
            collective_id=collective_id, has_side_effects=True, vmem_limit_bytes=32 * 2**20
        ),
    )(array)


def local(pair, valid_len, tri_in, tri_gate, tri_out, att_qkvg, att_bias, att_out):
    tile_rows, tile_cols, width = pair.shape
    n_row, n_col = lax.axis_size("row"), lax.axis_size("col")
    n = n_row * n_col
    tokens = n_col * tile_cols
    own_rows = tokens // n
    heads = att_bias.shape[1]
    head_dim = width // heads
    limit = valid_len[0]
    keep = jnp.arange(tokens) < limit
    row_keep = lax.dynamic_slice(keep, (lax.axis_index("row") * tile_rows,), (tile_rows,))
    col_keep = lax.dynamic_slice(keep, (lax.axis_index("col") * tile_cols,), (tile_cols,))
    mask = (row_keep[:, None] & col_keep[None, :]).astype(jnp.float32)

    pair_rows = exchange(pair.reshape(n_col, own_rows, tile_cols, width), n_col, n_col, 0, whole=False)
    pair_rows = jnp.swapaxes(pair_rows, 0, 1).reshape(own_rows, tokens, width).astype(jnp.float32)

    normed = layer_norm(pair.astype(jnp.float32), -1).astype(jnp.bfloat16)
    proj = jnp.einsum("cd,ikc->dik", tri_in, normed, preferred_element_type=jnp.float32)
    proj = proj.reshape(4, width, tile_rows, tile_cols)
    left = (jax.nn.sigmoid(proj[0]) * proj[1] * mask).astype(jnp.bfloat16)
    right = (jax.nn.sigmoid(proj[2]) * proj[3] * mask).astype(jnp.bfloat16)
    both = jnp.stack([left, right], axis=1).reshape(n, 2, -1, 128)
    both = exchange(both, n, n_col, 1)
    both = both.reshape(n_row, n_col, 2, tile_rows, tile_cols)
    both = jnp.transpose(both, (2, 0, 3, 1, 4)).reshape(2, tokens, tokens)
    product = jnp.einsum("ik,jk->ij", both[0], both[1], preferred_element_type=jnp.float32)
    product = exchange(product.astype(jnp.bfloat16).reshape(n, -1, 128), n, n_col, 2)
    product = product.reshape(width, own_rows, tokens).astype(jnp.float32)
    prodnorm = layer_norm(product, 0).astype(jnp.bfloat16)

    normed = layer_norm(pair_rows, -1).astype(jnp.bfloat16)
    tgate = jax.nn.sigmoid(jnp.dot(normed, tri_gate, preferred_element_type=jnp.float32))
    update = jnp.einsum("cij,cd->ijd", prodnorm, tri_out, preferred_element_type=jnp.float32)
    first = (pair_rows + tgate * update).astype(jnp.bfloat16).astype(jnp.float32)
    normed = layer_norm(first, -1).astype(jnp.bfloat16)
    bias = jnp.einsum("jkc,ch->hjk", normed, att_bias, preferred_element_type=jnp.float32)
    bias = bias.astype(jnp.bfloat16).reshape(heads * own_rows, tokens)
    bias = exchange(bias, n, n_col, 3, same=True)
    bias = jnp.transpose(bias.reshape(n, heads, own_rows, tokens), (1, 0, 2, 3))
    bias = bias.reshape(heads, tokens, tokens).astype(jnp.float32)

    qkvg = jnp.dot(normed, att_qkvg, preferred_element_type=jnp.float32)
    agate = jax.nn.sigmoid(qkvg[..., 3 * width :])
    qkv = qkvg[..., : 3 * width].astype(jnp.bfloat16)
    qkv = qkv.reshape(own_rows, tokens, 3, heads, head_dim)
    query, key, value = qkv[:, :, 0], qkv[:, :, 1], qkv[:, :, 2]
    scores = jnp.einsum("ijhd,ikhd->ihjk", query, key, preferred_element_type=jnp.float32)
    key_bias = jnp.where(keep, 0.0, -1000000000.0).astype(jnp.float32)
    scores = scores * head_dim ** (-0.5) + bias + key_bias
    expo = jnp.exp(scores - jnp.max(scores, axis=-1, keepdims=True))
    total = jnp.sum(expo, axis=-1)
    att = jnp.einsum(
        "ihjk,ikhd->ijhd", expo.astype(jnp.bfloat16), value, preferred_element_type=jnp.float32
    )
    att = att / jnp.swapaxes(total, 1, 2)[..., None]
    gated = (agate * att.reshape(own_rows, tokens, width)).astype(jnp.bfloat16)
    updated = first + jnp.dot(gated, att_out, preferred_element_type=jnp.float32)
    updated = updated.astype(jnp.bfloat16).reshape(own_rows, n_col, tile_cols, width)
    updated = exchange(jnp.swapaxes(updated, 0, 1), n_col, n_col, 4, whole=False)
    return updated.reshape(tile_rows, tile_cols, width)


def solution(mesh):
    placed = (P("row", "col", None), P(), P(), P(), P(), P(), P(), P())
    return jax.shard_map(
        local, mesh=mesh, in_specs=placed, out_specs=P("row", "col", None), check_vma=False
    )
```

```python
import functools

import jax
import jax.numpy as jnp
from jax import lax
from jax.experimental import pallas as pl
from jax.experimental.pallas import tpu as pltpu
from jax.sharding import PartitionSpec as P

MESH = pl.DeviceIdType.MESH
BF16, F32 = jnp.bfloat16, jnp.float32
N_ROW, N_COL, N_DEV, N_CHIP = 16, 8, 128, 64
ROWS, COLS, OWN, HALF, C = 32, 64, 8, 256, 128
HEADS, DH = 4, 32


def layer_norm(values, axis=-1):
    mean = jnp.mean(values, axis=axis, keepdims=True)
    centred = values - mean
    var = jnp.mean(centred * centred, axis=axis, keepdims=True)
    return centred * lax.rsqrt(var + 1e-05)


def sigmoid(values):
    return 0.5 * jnp.tanh(0.5 * values) + 0.5


def dot(a, b):
    return jnp.dot(a, b, preferred_element_type=F32)


def dot_t(a, b):
    return lax.dot_general(a, b, (((1,), (1,)), ((), ())), preferred_element_type=F32)


def wait(ref, sem):
    pltpu.make_async_copy(ref, ref, sem).wait()


def kernel(
    pair_ref, limit_ref, tri_in_ref, tri_gate_ref, tri_out_ref, qkvg_ref, abias_ref, aout_ref,
    out_ref,
    pair_v, zn, wt, stage, amsg, abuf, amat, xmsg, xbuf, xs, prow, tg, z1, yn, bmsg, bbuf,
    qx, kb, vb, ag, att, omsg,
    load_sem, pair_sem, a_sem, x_sem, yn_sem, b_send, b_recv, o_sem,
):
    r, q = lax.axis_index("row"), lax.axis_index("col")
    me = r * N_COL + q
    core = lax.rem(r, 2)
    chip = (r // 2) * N_COL + q
    part = chip // (N_CHIP // 2)
    limit = limit_ref[0]

    def at(device):
        return (device // N_COL, lax.rem(device, N_COL))

    def post(src, dst, send, recv, row, col):
        here = jnp.logical_and(row == r, col == q)

        @pl.when(here)
        def _():
            pltpu.make_async_copy(src, dst, recv).start()

        @pl.when(jnp.logical_not(here))
        def _():
            pltpu.make_async_remote_copy(
                src_ref=src, dst_ref=dst, send_sem=send, recv_sem=recv,
                device_id=(row, col), device_id_type=MESH,
            ).start()

    load = pltpu.make_async_copy(pair_ref, pair_v, load_sem)
    load.start()
    barrier = pltpu.get_barrier_semaphore()

    def greet(step, carry):
        pl.semaphore_signal(
            barrier, inc=1, device_id=at(lax.rem(me + step, N_DEV)), device_id_type=MESH
        )
        return carry

    lax.fori_loop(1, N_DEV, greet, 0)
    wt[...] = tri_in_ref[...].T
    load.wait()

    def norm_block(b, carry):
        v = pair_v[pl.ds(4 * b, 4)].astype(F32)
        zn[pl.ds(4 * lax.rem(b, 4), 4), b // 4] = layer_norm(v).astype(BF16)
        return carry

    lax.fori_loop(0, 8, norm_block, 0)
    pl.semaphore_wait(barrier, N_DEV - 1)

    for u in range(4):
        owner = 4 * r + u
        post(
            pair_v.at[pl.ds(8 * u, 8)], prow.at[:, lax.rem(q, 4)], pair_sem.at[0], pair_sem.at[1],
            2 * (owner // N_COL) + q // 4, lax.rem(owner, N_COL),
        )

    s_id = lax.broadcasted_iota(jnp.int32, (16, 128), 0)
    l_id = lax.broadcasted_iota(jnp.int32, (16, 128), 1)
    i_id = ROWS * r + 16 * (l_id // COLS) + s_id
    k_id = COLS * q + lax.rem(l_id, COLS)
    mask = jnp.where((i_id < limit) & (k_id < limit), 1.0, 0.0).astype(F32)

    def send_ab(n, carry):
        first = 32 * lax.rem(me // 32 + n, 4)
        weights = jnp.concatenate(
            [wt[pl.ds(pl.multiple_of(k * C + first, 32), 32)] for k in range(4)], axis=0
        )

        def gate(piece, inner):
            rhs = zn[pl.ds(4 * piece, 4)].reshape(512, C)
            proj = dot_t(weights, rhs)
            a = sigmoid(proj[0:32]) * proj[32:64]
            b = sigmoid(proj[64:96]) * proj[96:128]
            for k in range(4):
                s = 4 * piece + k
                stage[pl.ds(s, 32, stride=32)] = a[:, 128 * k : 128 * (k + 1)]
                stage[pl.ds(16 + s, 32, stride=32)] = b[:, 128 * k : 128 * (k + 1)]
            return inner

        lax.fori_loop(0, 4, gate, 0)
        both = stage[...].reshape(32, 2, 16, 128) * mask
        amsg[pl.ds(first, 32)] = both.astype(BF16)

        def send(w, inner):
            to = first + lax.rem(me + w, 32)
            post(amsg.at[to], abuf.at[r, q], a_sem.at[0], a_sem.at[1], *at(to))
            return inner

        lax.fori_loop(0, 32, send, 0)
        return carry

    lax.fori_loop(0, 4, send_ab, 0)

    wait(prow, pair_sem.at[1])

    def tri_gate(s, carry):
        v = prow[s].reshape(HALF, C).astype(F32)
        tg[s] = sigmoid(dot(layer_norm(v).astype(BF16), tri_gate_ref[...]))
        return carry

    lax.fori_loop(0, OWN, tri_gate, 0)

    wait(abuf, a_sem.at[1])
    for side in range(2):
        for u in range(4):
            even = abuf[:, 2 * u, side].reshape(256, 128)
            odd = abuf[:, 2 * u + 1, side].reshape(256, 128)
            low = jnp.concatenate([even[:, :64], odd[:, :64]], axis=1).reshape(16, 1, 16, 128)
            high = jnp.concatenate([even[:, 64:], odd[:, 64:]], axis=1).reshape(16, 1, 16, 128)
            amat[side, :, 128 * u : 128 * (u + 1)] = jnp.concatenate([low, high], axis=1).reshape(
                512, 128
            )

    def send_x(n, carry):
        g = lax.rem(me // 32 + n, 4)
        x = dot_t(amat[0, pl.ds(pl.multiple_of(128 * g, 128), 128)], amat[1]).reshape(2, 8, 8, 512)
        for mm in range(2):
            for c in range(2):
                tiles = [x[mm, :, :, 128 * t : 128 * (t + 1)] for t in (2 * c, 2 * c + 1)]
                xmsg[4 * g + 2 * mm + c] = jnp.concatenate(tiles, axis=1).astype(BF16)

        def send(w, inner):
            to = at(32 * g + lax.rem(me + w, 32))
            post(xmsg.at[to[0], to[1]], xbuf.at[me], x_sem.at[0], x_sem.at[1], *to)
            return inner

        lax.fori_loop(0, 32, send, 0)
        return carry

    lax.fori_loop(0, 4, send_x, 0)

    wait(xbuf, x_sem.at[1])
    xs[...] = layer_norm(xbuf[...].astype(F32), 0).reshape(2048, 128)
    for p in range(16):
        s, t = p % 8, p // 8
        xn = xs[pl.ds(p, 128, stride=16)].T.astype(BF16)
        update = dot(xn, tri_out_ref[...])
        v = prow[s, 2 * t : 2 * t + 2].reshape(128, C).astype(F32)
        first = (v + tg[s, 128 * t : 128 * (t + 1)] * update).astype(BF16)
        z1[s, 128 * t : 128 * (t + 1)] = first
        yn[core, s, 128 * t : 128 * (t + 1)] = layer_norm(first.astype(F32)).astype(BF16)

    share = pltpu.make_async_remote_copy(
        src_ref=yn.at[core], dst_ref=yn.at[core], send_sem=yn_sem.at[0], recv_sem=yn_sem.at[1],
        device_id=(r + 1 - 2 * core, q), device_id_type=MESH,
    )
    share.start()

    place = lax.rem(lax.broadcasted_iota(jnp.int32, (32, C), 0), 8)
    bias = jnp.zeros((32, HALF), F32)
    for s in range(OWN):
        weights = jnp.where(place == s, abias_ref[...].astype(F32), 0.0).astype(BF16)
        bias += dot_t(weights, yn[core, s])
    bmsg[...] = bias.astype(BF16).reshape(2, 16, HALF)
    for pairing in range(2):

        def send_bias(w, carry, pairing=pairing):
            to = lax.rem(chip + w, N_CHIP)
            post(
                bmsg.at[pairing], bbuf.at[pairing, core, lax.rem(chip, N_CHIP // 2)],
                b_send.at[pairing], b_recv.at[pairing],
                2 * (to // N_COL) + part, lax.rem(to, N_COL),
            )
            return carry

        lax.fori_loop(0, N_CHIP, send_bias, 0)

    lane_head = lax.broadcasted_iota(jnp.int32, (8, C), 1) // DH

    def own_qkvg(s, carry):
        qkvg = dot(yn[core, s], qkvg_ref[...])
        query = (qkvg[:, :C] * DH ** (-0.5)).reshape(32, 1, 8, C)
        for pairing in range(2):
            rows = [jnp.where(lane_head == 2 * pairing + h, query, 0.0) for h in range(2)]
            qx[pairing, s] = jnp.concatenate(rows, axis=1).reshape(512, C).astype(BF16)
        kb[core, s] = qkvg[:, C : 2 * C].astype(BF16)
        vb[core, s] = qkvg[:, 2 * C : 3 * C].astype(BF16)
        ag[s] = sigmoid(qkvg[:, 3 * C :])
        return carry

    lax.fori_loop(0, OWN, own_qkvg, 0)
    share.wait()

    def other_kv(s, carry):
        kv = dot(yn[1 - core, s], qkvg_ref[:, C : 3 * C])
        kb[1 - core, s] = kv[:, :C].astype(BF16)
        vb[1 - core, s] = kv[:, C:].astype(BF16)
        return carry

    lax.fori_loop(0, OWN, other_kv, 0)

    key_id = lax.broadcasted_iota(jnp.int32, (1, 2 * HALF), 1)
    key_bias = jnp.where(key_id < limit, 0.0, -1000000000.0).astype(F32)

    def attend(pairing, s):
        keys = kb[:, s].reshape(2 * HALF, C)
        vals = vb[:, s].reshape(2 * HALF, C)
        bias = jnp.concatenate([bbuf[pairing, 0], bbuf[pairing, 1]], axis=-1)
        scores = dot_t(qx[pairing, s], keys) + (
            bias.reshape(512, 2 * HALF).astype(F32) + key_bias
        )
        expo = jnp.exp(scores - jnp.max(scores, axis=-1, keepdims=True))
        total = jnp.sum(expo, axis=-1, keepdims=True)
        got = (dot(expo.astype(BF16), vals) / total).reshape(32, 2, 8, C)
        part0 = jnp.where(lane_head == 2 * pairing, got[:, 0], 0.0)
        return jnp.where(lane_head == 2 * pairing + 1, got[:, 1], part0).reshape(HALF, C)

    wait(bbuf.at[0], b_recv.at[0])

    def first_heads(s, carry):
        att[s] = attend(0, s)
        return carry

    lax.fori_loop(0, OWN, first_heads, 0)
    wait(bbuf.at[1], b_recv.at[1])

    def last_heads(s, carry):
        gated = (ag[s] * (att[s] + attend(1, s))).astype(BF16)
        done = z1[s].astype(F32) + dot(gated, aout_ref[...])
        omsg[s] = done.astype(BF16).reshape(4, COLS, C)
        for u in range(4):
            post(
                omsg.at[s, u], out_ref.at[8 * lax.rem(chip, 4) + s], o_sem.at[0], o_sem.at[1],
                chip // 4, 4 * core + u,
            )
        return carry

    lax.fori_loop(0, OWN, last_heads, 0)

    wait(amsg.at[pl.ds(0, N_DEV - 1)], a_sem.at[0])
    wait(xbuf.at[pl.ds(0, N_DEV - 1)], x_sem.at[0])
    own_block = core == q // 4
    own_bias = core == part

    @pl.when(own_block)
    def _():
        wait(prow.at[pl.ds(0, 6)], pair_sem.at[0])
        wait(prow.at[pl.ds(0, 6)], o_sem.at[0])

    @pl.when(jnp.logical_not(own_block))
    def _():
        wait(prow, pair_sem.at[0])
        wait(prow, o_sem.at[0])

    @pl.when(own_bias)
    def _():
        for pairing in range(2):
            wait(bbuf.at[pairing, 0], b_send.at[pairing])
            wait(bbuf.at[pairing, 1, pl.ds(0, 31)], b_send.at[pairing])

    @pl.when(jnp.logical_not(own_bias))
    def _():
        for pairing in range(2):
            wait(bbuf.at[pairing], b_send.at[pairing])

    wait(out_ref, o_sem.at[1])


def local(pair, valid_len, tri_in, tri_gate, tri_out, att_qkvg, att_bias, att_out):
    bias_rows = jnp.repeat(att_bias.T, OWN, axis=0)
    vmem = pl.BlockSpec(memory_space=pltpu.VMEM)
    hbm = pl.BlockSpec(memory_space=pl.ANY)
    smem = pl.BlockSpec(memory_space=pltpu.SMEM)
    dma = pltpu.SemaphoreType.DMA
    return pl.pallas_call(
        kernel,
        out_shape=jax.ShapeDtypeStruct(pair.shape, pair.dtype),
        in_specs=[hbm, smem] + [vmem] * 6,
        out_specs=hbm,
        scratch_shapes=[
            pltpu.VMEM((ROWS, COLS, C), BF16),
            pltpu.VMEM((16, 2, COLS, C), BF16),
            pltpu.VMEM((4 * C, C), BF16),
            pltpu.VMEM((1024, 128), F32),
            pltpu.VMEM((N_DEV, 2, 16, 128), BF16),
            pltpu.VMEM((N_ROW, N_COL, 2, 16, 128), BF16),
            pltpu.VMEM((2, 512, 512), BF16),
            pltpu.VMEM((N_ROW, N_COL, 16, 128), BF16),
            pltpu.VMEM((N_DEV, 16, 128), BF16),
            pltpu.VMEM((2048, 128), F32),
            pltpu.VMEM((OWN, 4, COLS, C), BF16),
            pltpu.VMEM((OWN, HALF, C), F32),
            pltpu.VMEM((OWN, HALF, C), BF16),
            pltpu.VMEM((2, OWN, HALF, C), BF16),
            pltpu.VMEM((2, 16, HALF), BF16),
            pltpu.VMEM((2, 2, N_CHIP // 2, 16, HALF), BF16),
            pltpu.VMEM((2, OWN, 512, C), BF16),
            pltpu.VMEM((2, OWN, HALF, C), BF16),
            pltpu.VMEM((2, OWN, HALF, C), BF16),
            pltpu.VMEM((OWN, HALF, C), F32),
            pltpu.VMEM((OWN, HALF, C), F32),
            pltpu.VMEM((OWN, 4, COLS, C), BF16),
            dma,
            dma((2,)),
            dma((2,)),
            dma((2,)),
            dma((2,)),
            dma((2,)),
            dma((2,)),
            dma((2,)),
        ],
        compiler_params=pltpu.CompilerParams(
            collective_id=0, has_side_effects=True, vmem_limit_bytes=40 * 2**20
        ),
        name="pairformer",
    )(pair, valid_len, tri_in, tri_gate, tri_out, att_qkvg, bias_rows, att_out)


def solution(mesh):
    placed = (P("row", "col", None), P(), P(), P(), P(), P(), P(), P())
    return jax.shard_map(
        local, mesh=mesh, in_specs=placed, out_specs=P("row", "col", None), check_vma=False
    )
```

```python
import itertools

import jax
import jax.numpy as jnp
from jax import lax
from jax.experimental import pallas as pl
from jax.experimental.pallas import tpu as pltpu
from jax.sharding import PartitionSpec as P

MESH = pl.DeviceIdType.MESH
BF16, F32 = jnp.bfloat16, jnp.float32
N_ROW, N_COL, N_DEV, N_CHIP = 16, 8, 128, 64
ROWS, COLS, OWN, HALF, C = 32, 64, 8, 256, 128
HEADS, DH = 4, 32


def layer_norm(values, axis=-1):
    mean = jnp.mean(values, axis=axis, keepdims=True)
    centred = values - mean
    var = jnp.mean(centred * centred, axis=axis, keepdims=True)
    return centred * lax.rsqrt(var + 1e-05)


def sigmoid(values):
    return 0.5 * jnp.tanh(0.5 * values) + 0.5


def dot(a, b):
    return jnp.dot(a, b, preferred_element_type=F32)


def dot_t(a, b):
    return lax.dot_general(a, b, (((1,), (1,)), ((), ())), preferred_element_type=F32)


def far_first(cores):
    ring = (0, 1, 2, 1)
    steps = itertools.product(range(4), range(4), range(4), cores)
    return sorted(steps, key=lambda d: -(ring[d[0]] + ring[d[1]] + ring[d[2]]))


def wait(ref, sem):
    pltpu.make_async_copy(ref, ref, sem).wait()


def kernel(
    pair_ref, limit_ref, tri_in_hbm, tri_gate_hbm, tri_out_hbm, qkvg_hbm, abias_hbm, aout_hbm,
    out_ref,
    tri_in_ref, tri_gate_ref, tri_out_ref, qkvg_ref, abias_ref, aout_ref,
    pair_v, zn, wt, stage, amsg, abuf, amat, xmsg, xbuf, xs, prow, tg, z1, yn, bmsg, bbuf,
    qx, kb, vb, ag, att, omsg,
    load_sem, pair_sem, a_sem, x_sem, yn_sem, b_send, b_recv, o_sem,
):
    r, q = lax.axis_index("row"), lax.axis_index("col")
    me = r * N_COL + q
    core = lax.rem(r, 2)
    chip = (r // 2) * N_COL + q
    part = chip // (N_CHIP // 2)
    limit = limit_ref[0]

    cx, cy, cz = 2 * (q // 4) + r // 8, lax.rem(q, 4), lax.rem(r // 2, 4)
    xs_at = [lax.rem(cx + d, 4) for d in range(4)]
    ys_at = [lax.rem(cy + d, 4) for d in range(4)]
    zs_at = [lax.rem(cz + d, 4) for d in range(4)]
    core_at = [core, 1 - core]
    quarter = lax.rem(cx + cy + cz, 4)
    channel = 32 * quarter + 8 * cx + 2 * cy + core

    def device(x, y, z, which):
        return 8 * lax.rem(x, 2) + 2 * z + which, 4 * (x // 2) + y

    def push(src, dst, send, recv, to):
        pltpu.make_async_remote_copy(
            src_ref=src, dst_ref=dst, send_sem=send, recv_sem=recv,
            device_id=to, device_id_type=MESH,
        ).start()

    def at(device):
        return (device // N_COL, lax.rem(device, N_COL))

    def post(src, dst, send, recv, row, col):
        here = jnp.logical_and(row == r, col == q)

        @pl.when(here)
        def _():
            pltpu.make_async_copy(src, dst, recv).start()

        @pl.when(jnp.logical_not(here))
        def _():
            pltpu.make_async_remote_copy(
                src_ref=src, dst_ref=dst, send_sem=send, recv_sem=recv,
                device_id=(row, col), device_id_type=MESH,
            ).start()

    loads = [
        pltpu.make_async_copy(src, dst, load_sem.at[k])
        for k, (src, dst) in enumerate(
            [
                (pair_ref, pair_v), (tri_in_hbm, tri_in_ref), (tri_gate_hbm, tri_gate_ref),
                (tri_out_hbm, tri_out_ref), (qkvg_hbm, qkvg_ref), (abias_hbm, abias_ref),
                (aout_hbm, aout_ref),
            ]
        )
    ]
    for load in loads:
        load.start()
    barrier = pltpu.get_barrier_semaphore()

    def greet(step, carry):
        pl.semaphore_signal(
            barrier, inc=1, device_id=at(lax.rem(me + step, N_DEV)), device_id_type=MESH
        )
        return carry

    lax.fori_loop(1, N_DEV, greet, 0)
    for load in loads:
        load.wait()
    wt[...] = tri_in_ref[...].T

    def norm_block(b, carry):
        v = pair_v[pl.ds(4 * b, 4)].astype(F32)
        zn[pl.ds(4 * lax.rem(b, 4), 4), b // 4] = layer_norm(v).astype(BF16)
        return carry

    lax.fori_loop(0, 8, norm_block, 0)
    pl.semaphore_wait(barrier, N_DEV - 1)

    for u in range(4):
        owner = 4 * r + u
        post(
            pair_v.at[pl.ds(8 * u, 8)], prow.at[:, lax.rem(q, 4)], pair_sem.at[0], pair_sem.at[1],
            2 * (owner // N_COL) + q // 4, lax.rem(owner, N_COL),
        )

    s_id = lax.broadcasted_iota(jnp.int32, (16, 128), 0)
    l_id = lax.broadcasted_iota(jnp.int32, (16, 128), 1)
    i_id = ROWS * r + 16 * (l_id // COLS) + s_id
    k_id = COLS * q + lax.rem(l_id, COLS)
    mask = jnp.where((i_id < limit) & (k_id < limit), 1.0, 0.0).astype(F32)

    planes = sorted(itertools.product(range(4), range(4)), key=lambda d: -(d[0] % 2 + d[1] % 2))

    def send_ab(n, carry):
        ahead = lax.rem(n + 1, 4)
        group = lax.rem(quarter + ahead, 4)
        first = 32 * group
        weights = jnp.concatenate(
            [wt[pl.ds(pl.multiple_of(k * C + first, 32), 32)] for k in range(4)], axis=0
        )

        def gate(piece, inner):
            rhs = zn[pl.ds(4 * piece, 4)].reshape(512, C)
            proj = dot_t(weights, rhs)
            a = sigmoid(proj[0:32]) * proj[32:64]
            b = sigmoid(proj[64:96]) * proj[96:128]
            for k in range(4):
                s = 4 * piece + k
                stage[pl.ds(s, 32, stride=32)] = a[:, 128 * k : 128 * (k + 1)]
                stage[pl.ds(16 + s, 32, stride=32)] = b[:, 128 * k : 128 * (k + 1)]
            return inner

        lax.fori_loop(0, 4, gate, 0)
        both = stage[...].reshape(32, 2, 16, 128) * mask
        amsg[pl.ds(first, 32)] = both.astype(BF16)

        for dx, dy in planes:
            tx, ty = xs_at[dx], ys_at[dy]
            tz = lax.rem(group + 8 - tx - ty, 4)
            for c in range(2):
                to = device(tx, ty, tz, core_at[c])
                src = amsg.at[first + 8 * tx + 2 * ty + core_at[c]]
                if (dx, dy, c) == (0, 0, 0):
                    post(src, abuf.at[r, q], a_sem.at[0], a_sem.at[1], *to)
                else:
                    push(src, abuf.at[r, q], a_sem.at[0], a_sem.at[1], to)
        return carry

    lax.fori_loop(0, 4, send_ab, 0)

    wait(prow, pair_sem.at[1])

    def tri_gate(s, carry):
        v = prow[s].reshape(HALF, C).astype(F32)
        tg[s] = sigmoid(dot(layer_norm(v).astype(BF16), tri_gate_ref[...]))
        return carry

    lax.fori_loop(0, OWN, tri_gate, 0)

    wait(abuf, a_sem.at[1])
    for side in range(2):
        for u in range(4):
            even = abuf[:, 2 * u, side].reshape(256, 128)
            odd = abuf[:, 2 * u + 1, side].reshape(256, 128)
            low = jnp.concatenate([even[:, :64], odd[:, :64]], axis=1).reshape(16, 1, 16, 128)
            high = jnp.concatenate([even[:, 64:], odd[:, 64:]], axis=1).reshape(16, 1, 16, 128)
            amat[side, :, 128 * u : 128 * (u + 1)] = jnp.concatenate([low, high], axis=1).reshape(
                512, 128
            )

    def product(g, carry):
        x = dot_t(amat[0, pl.ds(pl.multiple_of(128 * g, 128), 128)], amat[1]).reshape(2, 8, 8, 512)
        for mm in range(2):
            for c in range(2):
                tiles = [x[mm, :, :, 128 * t : 128 * (t + 1)] for t in (2 * c, 2 * c + 1)]
                xmsg[4 * g + 2 * mm + c] = jnp.concatenate(tiles, axis=1).astype(BF16)
        return carry

    lax.fori_loop(0, 4, product, 0)
    pltpu.make_async_copy(xmsg.at[r, q], xbuf.at[channel], x_sem.at[1]).start()
    for dx, dy, dz, c in far_first([0, 1]):
        if (dx, dy, dz, c) != (0, 0, 0, 0):
            to = device(xs_at[dx], ys_at[dy], zs_at[dz], core_at[c])
            push(xmsg.at[to[0], to[1]], xbuf.at[channel], x_sem.at[0], x_sem.at[1], to)

    wait(xbuf, x_sem.at[1])
    xs[...] = layer_norm(xbuf[...].astype(F32), 0).reshape(2048, 128)
    for p in range(16):
        s, t = p % 8, p // 8
        xn = xs[pl.ds(p, 128, stride=16)].T.astype(BF16)
        update = dot(xn, tri_out_ref[...])
        v = prow[s, 2 * t : 2 * t + 2].reshape(128, C).astype(F32)
        first = (v + tg[s, 128 * t : 128 * (t + 1)] * update).astype(BF16)
        z1[s, 128 * t : 128 * (t + 1)] = first
        yn[core, s, 128 * t : 128 * (t + 1)] = layer_norm(first.astype(F32)).astype(BF16)

    share = pltpu.make_async_remote_copy(
        src_ref=yn.at[core], dst_ref=yn.at[core], send_sem=yn_sem.at[0], recv_sem=yn_sem.at[1],
        device_id=(r + 1 - 2 * core, q), device_id_type=MESH,
    )
    share.start()

    place = lax.rem(lax.broadcasted_iota(jnp.int32, (32, C), 0), 8)
    columns = abias_ref[...].astype(F32)
    columns = jnp.concatenate(
        [jnp.broadcast_to(columns[h : h + 1], (8, C)) for h in range(HEADS)], axis=0
    )
    bias = jnp.zeros((32, HALF), F32)
    for s in range(OWN):
        weights = jnp.where(place == s, columns, 0.0).astype(BF16)
        bias += dot_t(weights, yn[core, s])
    bmsg[...] = bias.astype(BF16).reshape(2, 16, HALF)
    def send_bias(pairing):
        dst = bbuf.at[pairing, core, lax.rem(chip, N_CHIP // 2)]
        for dx, dy, dz, _ in far_first([0]):
            to = device(xs_at[dx], ys_at[dy], zs_at[dz], part)
            if (dx, dy, dz) == (0, 0, 0):
                post(bmsg.at[pairing], dst, b_send.at[pairing], b_recv.at[pairing], *to)
            else:
                push(bmsg.at[pairing], dst, b_send.at[pairing], b_recv.at[pairing], to)

    def bias_sent(pairing):
        own_bias = core == part

        @pl.when(own_bias)
        def _():
            wait(bbuf.at[pairing, 0], b_send.at[pairing])
            wait(bbuf.at[pairing, 1, pl.ds(0, 31)], b_send.at[pairing])

        @pl.when(jnp.logical_not(own_bias))
        def _():
            wait(bbuf.at[pairing], b_send.at[pairing])

    send_bias(0)

    lane_head = lax.broadcasted_iota(jnp.int32, (8, C), 1) // DH

    def own_qkvg(s, carry):
        qkvg = dot(yn[core, s], qkvg_ref[...])
        query = (qkvg[:, :C] * DH ** (-0.5)).reshape(32, 1, 8, C)
        for pairing in range(2):
            rows = [jnp.where(lane_head == 2 * pairing + h, query, 0.0) for h in range(2)]
            qx[pairing, s] = jnp.concatenate(rows, axis=1).reshape(512, C).astype(BF16)
        kb[core, s] = qkvg[:, C : 2 * C].astype(BF16)
        vb[core, s] = qkvg[:, 2 * C : 3 * C].astype(BF16)
        ag[s] = sigmoid(qkvg[:, 3 * C :])
        return carry

    lax.fori_loop(0, OWN, own_qkvg, 0)
    share.wait()

    def other_kv(s, carry):
        kv = dot(yn[1 - core, s], qkvg_ref[:, C : 3 * C])
        kb[1 - core, s] = kv[:, :C].astype(BF16)
        vb[1 - core, s] = kv[:, C:].astype(BF16)
        return carry

    lax.fori_loop(0, OWN, other_kv, 0)
    bias_sent(0)
    send_bias(1)

    key_id = lax.broadcasted_iota(jnp.int32, (1, 2 * HALF), 1)
    key_bias = jnp.where(key_id < limit, 0.0, -1000000000.0).astype(F32)

    def attend(pairing, s):
        keys = kb[:, s].reshape(2 * HALF, C)
        vals = vb[:, s].reshape(2 * HALF, C)
        bias = jnp.concatenate([bbuf[pairing, 0], bbuf[pairing, 1]], axis=-1)
        scores = dot_t(qx[pairing, s], keys) + (
            bias.reshape(512, 2 * HALF).astype(F32) + key_bias
        )
        expo = jnp.exp(scores - jnp.max(scores, axis=-1, keepdims=True))
        total = jnp.sum(expo, axis=-1, keepdims=True)
        got = (dot(expo.astype(BF16), vals) / total).reshape(32, 2, 8, C)
        part0 = jnp.where(lane_head == 2 * pairing, got[:, 0], 0.0)
        return jnp.where(lane_head == 2 * pairing + 1, got[:, 1], part0).reshape(HALF, C)

    wait(bbuf.at[0], b_recv.at[0])

    def first_heads(s, carry):
        att[s] = attend(0, s)
        return carry

    lax.fori_loop(0, OWN, first_heads, 0)
    wait(bbuf.at[1], b_recv.at[1])

    def last_heads(s, carry):
        gated = (ag[s] * (att[s] + attend(1, s))).astype(BF16)
        done = z1[s].astype(F32) + dot(gated, aout_ref[...])
        omsg[s] = done.astype(BF16).reshape(4, COLS, C)
        for u in range(4):
            post(
                omsg.at[s, u], out_ref.at[8 * lax.rem(chip, 4) + s], o_sem.at[0], o_sem.at[1],
                chip // 4, 4 * core + u,
            )
        return carry

    lax.fori_loop(0, OWN, last_heads, 0)

    wait(amsg.at[pl.ds(0, N_DEV - 1)], a_sem.at[0])
    wait(xbuf.at[pl.ds(0, N_DEV - 1)], x_sem.at[0])
    own_block = core == q // 4
    @pl.when(own_block)
    def _():
        wait(prow.at[pl.ds(0, 6)], pair_sem.at[0])
        wait(prow.at[pl.ds(0, 6)], o_sem.at[0])

    @pl.when(jnp.logical_not(own_block))
    def _():
        wait(prow, pair_sem.at[0])
        wait(prow, o_sem.at[0])

    bias_sent(1)
    wait(out_ref, o_sem.at[1])


def local(pair, valid_len, tri_in, tri_gate, tri_out, att_qkvg, att_bias, att_out):
    hbm = pl.BlockSpec(memory_space=pltpu.HBM)
    smem = pl.BlockSpec(memory_space=pltpu.SMEM)
    dma = pltpu.SemaphoreType.DMA
    return pl.pallas_call(
        kernel,
        out_shape=jax.ShapeDtypeStruct(pair.shape, pair.dtype),
        in_specs=[hbm, smem] + [hbm] * 6,
        out_specs=hbm,
        scratch_shapes=[
            pltpu.VMEM(tri_in.shape, BF16),
            pltpu.VMEM(tri_gate.shape, BF16),
            pltpu.VMEM(tri_out.shape, BF16),
            pltpu.VMEM(att_qkvg.shape, BF16),
            pltpu.VMEM(att_bias.shape[::-1], BF16),
            pltpu.VMEM(att_out.shape, BF16),
            pltpu.VMEM((ROWS, COLS, C), BF16),
            pltpu.VMEM((16, 2, COLS, C), BF16),
            pltpu.VMEM((4 * C, C), BF16),
            pltpu.VMEM((1024, 128), F32),
            pltpu.VMEM((N_DEV, 2, 16, 128), BF16),
            pltpu.VMEM((N_ROW, N_COL, 2, 16, 128), BF16),
            pltpu.VMEM((2, 512, 512), BF16),
            pltpu.VMEM((N_ROW, N_COL, 16, 128), BF16),
            pltpu.VMEM((N_DEV, 16, 128), BF16),
            pltpu.VMEM((2048, 128), F32),
            pltpu.VMEM((OWN, 4, COLS, C), BF16),
            pltpu.VMEM((OWN, HALF, C), F32),
            pltpu.VMEM((OWN, HALF, C), BF16),
            pltpu.VMEM((2, OWN, HALF, C), BF16),
            pltpu.VMEM((2, 16, HALF), BF16),
            pltpu.VMEM((2, 2, N_CHIP // 2, 16, HALF), BF16),
            pltpu.VMEM((2, OWN, 512, C), BF16),
            pltpu.VMEM((2, OWN, HALF, C), BF16),
            pltpu.VMEM((2, OWN, HALF, C), BF16),
            pltpu.VMEM((OWN, HALF, C), F32),
            pltpu.VMEM((OWN, HALF, C), F32),
            pltpu.VMEM((OWN, 4, COLS, C), BF16),
            dma((7,)),
            dma((2,)),
            dma((2,)),
            dma((2,)),
            dma((2,)),
            dma((2,)),
            dma((2,)),
            dma((2,)),
        ],
        compiler_params=pltpu.CompilerParams(
            collective_id=0, has_side_effects=True, vmem_limit_bytes=63 * 2**20
        ),
        name="pairformer",
    )(pair, valid_len, tri_in, tri_gate, tri_out, att_qkvg, att_bias.T, att_out)


def solution(mesh):
    placed = (P("row", "col", None), P(), P(), P(), P(), P(), P(), P())
    return jax.shard_map(
        local, mesh=mesh, in_specs=placed, out_specs=P("row", "col", None), check_vma=False
    )
```

```python
import itertools

import jax
import jax.numpy as jnp
from jax import lax
from jax.experimental import pallas as pl
from jax.experimental.pallas import tpu as pltpu
from jax.sharding import PartitionSpec as P

MESH = pl.DeviceIdType.MESH
BF16, F32 = jnp.bfloat16, jnp.float32
N_ROW, N_COL, N_DEV, N_CHIP = 16, 8, 128, 64
ROWS, COLS, OWN, HALF, C = 32, 64, 8, 256, 128
HEADS, DH = 4, 32


def layer_norm(values, axis=-1):
    mean = jnp.mean(values, axis=axis, keepdims=True)
    centred = values - mean
    var = jnp.mean(centred * centred, axis=axis, keepdims=True)
    return centred * lax.rsqrt(var + 1e-05)


def sigmoid(values):
    return 0.5 * jnp.tanh(0.5 * values) + 0.5


def dot(a, b):
    return jnp.dot(a, b, preferred_element_type=F32)


def dot_t(a, b):
    return lax.dot_general(a, b, (((1,), (1,)), ((), ())), preferred_element_type=F32)


def far_first(cores):
    ring = (0, 1, 2, 1)
    steps = itertools.product(range(4), range(4), range(4), cores)
    return sorted(steps, key=lambda d: -(ring[d[0]] + ring[d[1]] + ring[d[2]]))


def wait(ref, sem):
    pltpu.make_async_copy(ref, ref, sem).wait()


def kernel(
    pair_ref, limit_ref, tri_in_hbm, tri_gate_hbm, tri_out_hbm, qkvg_hbm, abias_hbm, aout_hbm,
    out_ref,
    tri_in_ref, tri_gate_ref, tri_out_ref, qkvg_ref, abias_ref, aout_ref,
    pair_v, zn, wt, stage, amsg, abuf, amat, xmsg, xbuf, xs, prow, tg, z1, yn, bmsg, bbuf,
    qx, kb, vb, ag, att, omsg,
    load_sem, in_sem, pair_sem, a_sem, x_sem, yn_sem, b_send, b_recv, o_sem,
):
    r, q = lax.axis_index("row"), lax.axis_index("col")
    me = r * N_COL + q
    core = lax.rem(r, 2)
    chip = (r // 2) * N_COL + q
    part = chip // (N_CHIP // 2)
    limit = limit_ref[0]

    cx, cy, cz = 2 * (q // 4) + r // 8, lax.rem(q, 4), lax.rem(r // 2, 4)
    xs_at = [lax.rem(cx + d, 4) for d in range(4)]
    ys_at = [lax.rem(cy + d, 4) for d in range(4)]
    zs_at = [lax.rem(cz + d, 4) for d in range(4)]
    core_at = [core, 1 - core]
    quarter = lax.rem(cx + cy + cz, 4)
    channel = 32 * quarter + 8 * cx + 2 * cy + core

    def device(x, y, z, which):
        return 8 * lax.rem(x, 2) + 2 * z + which, 4 * (x // 2) + y

    def push(src, dst, send, recv, to):
        pltpu.make_async_remote_copy(
            src_ref=src, dst_ref=dst, send_sem=send, recv_sem=recv,
            device_id=to, device_id_type=MESH,
        ).start()

    def at(device):
        return (device // N_COL, lax.rem(device, N_COL))

    def post(src, dst, send, recv, row, col):
        here = jnp.logical_and(row == r, col == q)

        @pl.when(here)
        def _():
            pltpu.make_async_copy(src, dst, recv).start()

        @pl.when(jnp.logical_not(here))
        def _():
            pltpu.make_async_remote_copy(
                src_ref=src, dst_ref=dst, send_sem=send, recv_sem=recv,
                device_id=(row, col), device_id_type=MESH,
            ).start()

    loads = [
        pltpu.make_async_copy(src, dst, load_sem.at[k])
        for k, (src, dst) in enumerate(
            [
                (pair_ref, pair_v), (tri_in_hbm, tri_in_ref), (tri_gate_hbm, tri_gate_ref),
                (tri_out_hbm, tri_out_ref), (qkvg_hbm, qkvg_ref), (abias_hbm, abias_ref),
                (aout_hbm, aout_ref),
            ]
        )
    ]
    for load in loads:
        load.start()
    barrier = pltpu.get_barrier_semaphore()
    mates = [(2 * (r // 2) + core_at[c], lax.rem(q + k, N_COL)) for c in range(2) for k in range(N_COL)]
    peers = [(lax.rem(r + 2 * k, N_ROW), q) for k in range(1, N_ROW // 2)]
    for to in mates[1:] + peers:
        pl.semaphore_signal(barrier, inc=1, device_id=to, device_id_type=MESH)
    for load in loads:
        load.wait()
    pl.semaphore_wait(barrier, len(mates) - 1 + len(peers))
    for to in peers:
        pl.semaphore_signal(in_sem, inc=1, device_id=to, device_id_type=MESH)
    for u in range(4):
        owner = 4 * r + u
        post(
            pair_v.at[pl.ds(8 * u, 8)], prow.at[:, lax.rem(q, 4)], pair_sem.at[0], pair_sem.at[1],
            2 * (owner // N_COL) + q // 4, lax.rem(owner, N_COL),
        )

    wt[...] = tri_in_ref[...].T

    def norm_block(b, carry):
        v = pair_v[pl.ds(4 * b, 4)].astype(F32)
        zn[pl.ds(4 * lax.rem(b, 4), 4), b // 4] = layer_norm(v).astype(BF16)
        return carry

    lax.fori_loop(0, 8, norm_block, 0)
    pl.semaphore_wait(in_sem, len(peers))

    s_id = lax.broadcasted_iota(jnp.int32, (16, 128), 0)
    l_id = lax.broadcasted_iota(jnp.int32, (16, 128), 1)
    i_id = ROWS * r + 16 * (l_id // COLS) + s_id
    k_id = COLS * q + lax.rem(l_id, COLS)
    mask = jnp.where((i_id < limit) & (k_id < limit), 1.0, 0.0).astype(F32)

    planes = sorted(itertools.product(range(4), range(4)), key=lambda d: -(d[0] % 2 + d[1] % 2))

    def send_ab(n, carry):
        ahead = lax.rem(n + 1, 4)
        group = lax.rem(quarter + ahead, 4)
        first = 32 * group
        weights = jnp.concatenate(
            [wt[pl.ds(pl.multiple_of(k * C + first, 32), 32)] for k in range(4)], axis=0
        )

        def gate(piece, inner):
            rhs = zn[pl.ds(4 * piece, 4)].reshape(512, C)
            proj = dot_t(weights, rhs)
            a = sigmoid(proj[0:32]) * proj[32:64]
            b = sigmoid(proj[64:96]) * proj[96:128]
            for k in range(4):
                s = 4 * piece + k
                stage[pl.ds(s, 32, stride=32)] = a[:, 128 * k : 128 * (k + 1)]
                stage[pl.ds(16 + s, 32, stride=32)] = b[:, 128 * k : 128 * (k + 1)]
            return inner

        lax.fori_loop(0, 4, gate, 0)
        both = stage[...].reshape(32, 2, 16, 128) * mask
        amsg[pl.ds(first, 32)] = both.astype(BF16)

        for dx, dy in planes:
            tx, ty = xs_at[dx], ys_at[dy]
            tz = lax.rem(group + 8 - tx - ty, 4)
            for c in range(2):
                to = device(tx, ty, tz, core_at[c])
                src = amsg.at[first + 8 * tx + 2 * ty + core_at[c]]
                if (dx, dy, c) == (0, 0, 0):
                    post(src, abuf.at[r, q], a_sem.at[0], a_sem.at[1], *to)
                else:
                    push(src, abuf.at[r, q], a_sem.at[0], a_sem.at[1], to)
        return carry

    lax.fori_loop(0, 4, send_ab, 0)

    wait(prow, pair_sem.at[1])

    def tri_gate(s, carry):
        v = prow[s].reshape(HALF, C).astype(F32)
        tg[s] = sigmoid(dot(layer_norm(v).astype(BF16), tri_gate_ref[...]))
        return carry

    lax.fori_loop(0, OWN, tri_gate, 0)

    wait(abuf, a_sem.at[1])
    for side in range(2):
        for u in range(4):
            even = abuf[:, 2 * u, side].reshape(256, 128)
            odd = abuf[:, 2 * u + 1, side].reshape(256, 128)
            low = jnp.concatenate([even[:, :64], odd[:, :64]], axis=1).reshape(16, 1, 16, 128)
            high = jnp.concatenate([even[:, 64:], odd[:, 64:]], axis=1).reshape(16, 1, 16, 128)
            amat[side, :, 128 * u : 128 * (u + 1)] = jnp.concatenate([low, high], axis=1).reshape(
                512, 128
            )

    def product(g, carry):
        x = dot_t(amat[0, pl.ds(pl.multiple_of(128 * g, 128), 128)], amat[1]).reshape(2, 8, 8, 512)
        for mm in range(2):
            for c in range(2):
                tiles = [x[mm, :, :, 128 * t : 128 * (t + 1)] for t in (2 * c, 2 * c + 1)]
                xmsg[4 * g + 2 * mm + c] = jnp.concatenate(tiles, axis=1).astype(BF16)
        return carry

    lax.fori_loop(0, 4, product, 0)
    pltpu.make_async_copy(xmsg.at[r, q], xbuf.at[channel], x_sem.at[1]).start()
    for dx, dy, dz, c in far_first([0, 1]):
        if (dx, dy, dz, c) != (0, 0, 0, 0):
            to = device(xs_at[dx], ys_at[dy], zs_at[dz], core_at[c])
            push(xmsg.at[to[0], to[1]], xbuf.at[channel], x_sem.at[0], x_sem.at[1], to)

    wait(xbuf, x_sem.at[1])
    xs[...] = layer_norm(xbuf[...].astype(F32), 0).reshape(2048, 128)
    for p in range(16):
        s, t = p % 8, p // 8
        xn = xs[pl.ds(p, 128, stride=16)].T.astype(BF16)
        update = dot(xn, tri_out_ref[...])
        v = prow[s, 2 * t : 2 * t + 2].reshape(128, C).astype(F32)
        first = (v + tg[s, 128 * t : 128 * (t + 1)] * update).astype(BF16)
        z1[s, 128 * t : 128 * (t + 1)] = first
        yn[core, s, 128 * t : 128 * (t + 1)] = layer_norm(first.astype(F32)).astype(BF16)

    share = pltpu.make_async_remote_copy(
        src_ref=yn.at[core], dst_ref=yn.at[core], send_sem=yn_sem.at[0], recv_sem=yn_sem.at[1],
        device_id=(r + 1 - 2 * core, q), device_id_type=MESH,
    )
    share.start()

    place = lax.rem(lax.broadcasted_iota(jnp.int32, (32, C), 0), 8)
    columns = abias_ref[...].astype(F32)
    columns = jnp.concatenate(
        [jnp.broadcast_to(columns[h : h + 1], (8, C)) for h in range(HEADS)], axis=0
    )
    bias = jnp.zeros((32, HALF), F32)
    for s in range(OWN):
        weights = jnp.where(place == s, columns, 0.0).astype(BF16)
        bias += dot_t(weights, yn[core, s])
    bmsg[...] = bias.astype(BF16).reshape(2, 16, HALF)
    def send_bias(pairing):
        dst = bbuf.at[pairing, core, lax.rem(chip, N_CHIP // 2)]
        for dx, dy, dz, _ in far_first([0]):
            to = device(xs_at[dx], ys_at[dy], zs_at[dz], part)
            if (dx, dy, dz) == (0, 0, 0):
                post(bmsg.at[pairing], dst, b_send.at[pairing], b_recv.at[pairing], *to)
            else:
                push(bmsg.at[pairing], dst, b_send.at[pairing], b_recv.at[pairing], to)

    def bias_sent(pairing):
        own_bias = core == part

        @pl.when(own_bias)
        def _():
            wait(bbuf.at[pairing, 0], b_send.at[pairing])
            wait(bbuf.at[pairing, 1, pl.ds(0, 31)], b_send.at[pairing])

        @pl.when(jnp.logical_not(own_bias))
        def _():
            wait(bbuf.at[pairing], b_send.at[pairing])

    send_bias(0)

    lane_head = lax.broadcasted_iota(jnp.int32, (8, C), 1) // DH

    def own_qkvg(s, carry):
        qkvg = dot(yn[core, s], qkvg_ref[...])
        query = (qkvg[:, :C] * DH ** (-0.5)).reshape(32, 1, 8, C)
        for pairing in range(2):
            rows = [jnp.where(lane_head == 2 * pairing + h, query, 0.0) for h in range(2)]
            qx[pairing, s] = jnp.concatenate(rows, axis=1).reshape(512, C).astype(BF16)
        kb[core, s] = qkvg[:, C : 2 * C].astype(BF16)
        vb[core, s] = qkvg[:, 2 * C : 3 * C].astype(BF16)
        ag[s] = sigmoid(qkvg[:, 3 * C :])
        return carry

    lax.fori_loop(0, OWN, own_qkvg, 0)
    share.wait()

    def other_kv(s, carry):
        kv = dot(yn[1 - core, s], qkvg_ref[:, C : 3 * C])
        kb[1 - core, s] = kv[:, :C].astype(BF16)
        vb[1 - core, s] = kv[:, C:].astype(BF16)
        return carry

    lax.fori_loop(0, OWN, other_kv, 0)
    bias_sent(0)
    send_bias(1)

    key_id = lax.broadcasted_iota(jnp.int32, (1, 2 * HALF), 1)
    key_bias = jnp.where(key_id < limit, 0.0, -1000000000.0).astype(F32)

    def attend(pairing, s):
        keys = kb[:, s].reshape(2 * HALF, C)
        vals = vb[:, s].reshape(2 * HALF, C)
        bias = jnp.concatenate([bbuf[pairing, 0], bbuf[pairing, 1]], axis=-1)
        scores = dot_t(qx[pairing, s], keys) + (
            bias.reshape(512, 2 * HALF).astype(F32) + key_bias
        )
        expo = jnp.exp(scores - jnp.max(scores, axis=-1, keepdims=True))
        total = jnp.sum(expo, axis=-1, keepdims=True)
        got = (dot(expo.astype(BF16), vals) / total).reshape(32, 2, 8, C)
        part0 = jnp.where(lane_head == 2 * pairing, got[:, 0], 0.0)
        return jnp.where(lane_head == 2 * pairing + 1, got[:, 1], part0).reshape(HALF, C)

    wait(bbuf.at[0], b_recv.at[0])

    def first_heads(s, carry):
        att[s] = attend(0, s)
        return carry

    lax.fori_loop(0, OWN, first_heads, 0)
    wait(bbuf.at[1], b_recv.at[1])

    def last_heads(s, carry):
        gated = (ag[s] * (att[s] + attend(1, s))).astype(BF16)
        done = z1[s].astype(F32) + dot(gated, aout_ref[...])
        omsg[s] = done.astype(BF16).reshape(4, COLS, C)
        for u in range(4):
            post(
                omsg.at[s, u], out_ref.at[8 * lax.rem(chip, 4) + s], o_sem.at[0], o_sem.at[1],
                chip // 4, 4 * core + u,
            )
        return carry

    lax.fori_loop(0, OWN, last_heads, 0)

    wait(amsg.at[pl.ds(0, N_DEV - 1)], a_sem.at[0])
    wait(xbuf.at[pl.ds(0, N_DEV - 1)], x_sem.at[0])
    own_block = core == q // 4
    @pl.when(own_block)
    def _():
        wait(prow.at[pl.ds(0, 6)], pair_sem.at[0])
        wait(prow.at[pl.ds(0, 6)], o_sem.at[0])

    @pl.when(jnp.logical_not(own_block))
    def _():
        wait(prow, pair_sem.at[0])
        wait(prow, o_sem.at[0])

    bias_sent(1)
    wait(out_ref, o_sem.at[1])


def local(pair, valid_len, tri_in, tri_gate, tri_out, att_qkvg, att_bias, att_out):
    hbm = pl.BlockSpec(memory_space=pltpu.HBM)
    smem = pl.BlockSpec(memory_space=pltpu.SMEM)
    dma = pltpu.SemaphoreType.DMA
    return pl.pallas_call(
        kernel,
        out_shape=jax.ShapeDtypeStruct(pair.shape, pair.dtype),
        in_specs=[hbm, smem] + [hbm] * 6,
        out_specs=hbm,
        scratch_shapes=[
            pltpu.VMEM(tri_in.shape, BF16),
            pltpu.VMEM(tri_gate.shape, BF16),
            pltpu.VMEM(tri_out.shape, BF16),
            pltpu.VMEM(att_qkvg.shape, BF16),
            pltpu.VMEM(att_bias.shape[::-1], BF16),
            pltpu.VMEM(att_out.shape, BF16),
            pltpu.VMEM((ROWS, COLS, C), BF16),
            pltpu.VMEM((16, 2, COLS, C), BF16),
            pltpu.VMEM((4 * C, C), BF16),
            pltpu.VMEM((1024, 128), F32),
            pltpu.VMEM((N_DEV, 2, 16, 128), BF16),
            pltpu.VMEM((N_ROW, N_COL, 2, 16, 128), BF16),
            pltpu.VMEM((2, 512, 512), BF16),
            pltpu.VMEM((N_ROW, N_COL, 16, 128), BF16),
            pltpu.VMEM((N_DEV, 16, 128), BF16),
            pltpu.VMEM((2048, 128), F32),
            pltpu.VMEM((OWN, 4, COLS, C), BF16),
            pltpu.VMEM((OWN, HALF, C), F32),
            pltpu.VMEM((OWN, HALF, C), BF16),
            pltpu.VMEM((2, OWN, HALF, C), BF16),
            pltpu.VMEM((2, 16, HALF), BF16),
            pltpu.VMEM((2, 2, N_CHIP // 2, 16, HALF), BF16),
            pltpu.VMEM((2, OWN, 512, C), BF16),
            pltpu.VMEM((2, OWN, HALF, C), BF16),
            pltpu.VMEM((2, OWN, HALF, C), BF16),
            pltpu.VMEM((OWN, HALF, C), F32),
            pltpu.VMEM((OWN, HALF, C), F32),
            pltpu.VMEM((OWN, 4, COLS, C), BF16),
            dma((7,)),
            pltpu.SemaphoreType.REGULAR,
            dma((2,)),
            dma((2,)),
            dma((2,)),
            dma((2,)),
            dma((2,)),
            dma((2,)),
            dma((2,)),
        ],
        compiler_params=pltpu.CompilerParams(
            collective_id=0, has_side_effects=True, vmem_limit_bytes=63 * 2**20
        ),
        name="pairformer",
    )(pair, valid_len, tri_in, tri_gate, tri_out, att_qkvg, att_bias.T, att_out)


def solution(mesh):
    placed = (P("row", "col", None), P(), P(), P(), P(), P(), P(), P())
    return jax.shard_map(
        local, mesh=mesh, in_specs=placed, out_specs=P("row", "col", None), check_vma=False
    )
```

```python
import itertools

import jax
import jax.numpy as jnp
from jax import lax
from jax.experimental import pallas as pl
from jax.experimental.pallas import tpu as pltpu
from jax.sharding import PartitionSpec as P

MESH = pl.DeviceIdType.MESH
BF16, F32 = jnp.bfloat16, jnp.float32
N_ROW, N_COL, N_DEV, N_CHIP = 16, 8, 128, 64
ROWS, COLS, OWN, HALF, C = 32, 64, 8, 256, 128
HEADS, DH = 4, 32


def layer_norm(values, axis=-1):
    mean = jnp.mean(values, axis=axis, keepdims=True)
    centred = values - mean
    var = jnp.mean(centred * centred, axis=axis, keepdims=True)
    return centred * lax.rsqrt(var + 1e-05)


def sigmoid(values):
    return 0.5 * jnp.tanh(0.5 * values) + 0.5


def dot(a, b):
    return jnp.dot(a, b, preferred_element_type=F32)


def dot_t(a, b):
    return lax.dot_general(a, b, (((1,), (1,)), ((), ())), preferred_element_type=F32)


def far_first(cores):
    ring = (0, 1, 2, 1)
    steps = itertools.product(range(4), range(4), range(4), cores)
    return sorted(steps, key=lambda d: -(ring[d[0]] + ring[d[1]] + ring[d[2]]))


def wait(ref, sem):
    pltpu.make_async_copy(ref, ref, sem).wait()


def kernel(
    pair_ref, limit_ref, tri_in_hbm, tri_gate_hbm, tri_out_hbm, qkvg_hbm, abias_hbm, aout_hbm,
    out_ref,
    tri_in_ref, tri_gate_ref, tri_out_ref, qkvg_ref, abias_ref, aout_ref,
    pair_v, zn, wt, stage, amsg, abuf, amat, xmsg, xbuf, xs, prow, tg, z1, yn, bmsg, bbuf,
    qx, kb, vb, ag, omsg,
    load_sem, in_sem, pair_sem, a_sem, x_sem, yn_sem, b_send, b_recv, o_sem,
):
    r, q = lax.axis_index("row"), lax.axis_index("col")
    me = r * N_COL + q
    core = lax.rem(r, 2)
    chip = (r // 2) * N_COL + q
    part = chip // (N_CHIP // 2)
    limit = limit_ref[0]
    flip = lax.rem(q, 4) // 2

    cx, cy, cz = 2 * (q // 4) + r // 8, lax.rem(q, 4), lax.rem(r // 2, 4)
    xs_at = [lax.rem(cx + d, 4) for d in range(4)]
    ys_at = [lax.rem(cy + d, 4) for d in range(4)]
    zs_at = [lax.rem(cz + d, 4) for d in range(4)]
    core_at = [core, 1 - core]
    quarter = lax.rem(cx + cy + cz, 4)
    channel = 32 * quarter + 8 * cx + 2 * cy + core

    def device(x, y, z, which):
        return 8 * lax.rem(x, 2) + 2 * z + which, 4 * (x // 2) + y

    def push(src, dst, send, recv, to):
        pltpu.make_async_remote_copy(
            src_ref=src, dst_ref=dst, send_sem=send, recv_sem=recv,
            device_id=to, device_id_type=MESH,
        ).start()

    def at(device):
        return (device // N_COL, lax.rem(device, N_COL))

    def post(src, dst, send, recv, row, col):
        here = jnp.logical_and(row == r, col == q)

        @pl.when(here)
        def _():
            pltpu.make_async_copy(src, dst, recv).start()

        @pl.when(jnp.logical_not(here))
        def _():
            pltpu.make_async_remote_copy(
                src_ref=src, dst_ref=dst, send_sem=send, recv_sem=recv,
                device_id=(row, col), device_id_type=MESH,
            ).start()

    loads = [
        pltpu.make_async_copy(src, dst, load_sem.at[k])
        for k, (src, dst) in enumerate(
            [
                (pair_ref, pair_v), (tri_in_hbm, tri_in_ref), (tri_gate_hbm, tri_gate_ref),
                (tri_out_hbm, tri_out_ref), (qkvg_hbm, qkvg_ref), (abias_hbm, abias_ref),
                (aout_hbm, aout_ref),
            ]
        )
    ]
    for load in loads:
        load.start()
    barrier = pltpu.get_barrier_semaphore()
    mates = [(2 * (r // 2) + core_at[c], lax.rem(q + k, N_COL)) for c in range(2) for k in range(N_COL)]
    peers = [(lax.rem(r + 2 * k, N_ROW), q) for k in range(1, N_ROW // 2)]
    for to in mates[1:] + peers:
        pl.semaphore_signal(barrier, inc=1, device_id=to, device_id_type=MESH)
    for load in loads:
        load.wait()
    pl.semaphore_wait(barrier, len(mates) - 1 + len(peers))
    for to in peers:
        pl.semaphore_signal(in_sem, inc=1, device_id=to, device_id_type=MESH)
    for k in (6, 2, 5, 7, 3, 1, 4, 0):
        col = lax.rem(q + k, N_COL)
        slot = 4 * lax.rem(core + lax.rem(col, 4) // 2, 2)
        src = pair_v.at[pl.ds(4 * col, 4)]
        dst = prow.at[pl.ds(slot, 4), lax.rem(q, 4)]
        post(src, dst, pair_sem.at[0], pair_sem.at[1], 2 * (r // 2) + q // 4, col)

    wt[...] = tri_in_ref[...].T

    def norm_block(b, carry):
        v = pair_v[pl.ds(4 * b, 4)].astype(F32)
        zn[pl.ds(4 * lax.rem(b, 4), 4), b // 4] = layer_norm(v).astype(BF16)
        return carry

    lax.fori_loop(0, 8, norm_block, 0)
    pl.semaphore_wait(in_sem, len(peers))

    s_id = lax.broadcasted_iota(jnp.int32, (16, 128), 0)
    l_id = lax.broadcasted_iota(jnp.int32, (16, 128), 1)
    k_id = COLS * q + lax.rem(l_id, COLS)
    quad = s_id // 4 + core * (1 - 2 * lax.rem(s_id // 4, 2))
    quad = 2 * lax.rem(quad, 2) + quad // 2

    def masked(s_order):
        i_id = ROWS * r + 16 * (l_id // COLS) + s_order
        return jnp.where((i_id < limit) & (k_id < limit), 1.0, 0.0).astype(F32)

    mask = jnp.stack([masked(4 * quad + lax.rem(s_id, 4)), masked(s_id)])

    planes = sorted(itertools.product(range(4), range(4)), key=lambda d: -(d[0] % 2 + d[1] % 2))

    def send_ab(n, carry):
        ahead = lax.rem(n + 1, 4)
        group = lax.rem(quarter + ahead, 4)
        first = 32 * group
        weights = jnp.concatenate(
            [wt[pl.ds(pl.multiple_of(k * C + first, 32), 32)] for k in range(4)], axis=0
        )

        def gate(piece, inner):
            rhs = zn[pl.ds(4 * piece, 4)].reshape(512, C)
            proj = dot_t(weights, rhs)
            a = sigmoid(proj[0:32]) * proj[32:64]
            b = sigmoid(proj[64:96]) * proj[96:128]
            swapped = 2 * lax.rem(piece, 2) + piece // 2
            place = 4 * (swapped + core * (1 - 2 * lax.rem(swapped, 2)))
            for k in range(4):
                stage[pl.ds(place + k, 32, stride=32)] = a[:, 128 * k : 128 * (k + 1)]
                stage[pl.ds(16 + 4 * piece + k, 32, stride=32)] = b[:, 128 * k : 128 * (k + 1)]
            return inner

        lax.fori_loop(0, 4, gate, 0)
        both = stage[...].reshape(32, 2, 16, 128) * mask
        amsg[pl.ds(first, 32)] = both.astype(BF16)

        for dx, dy in planes:
            tx, ty = xs_at[dx], ys_at[dy]
            tz = lax.rem(group + 8 - tx - ty, 4)
            for c in range(2):
                to = device(tx, ty, tz, core_at[c])
                src = amsg.at[first + 8 * tx + 2 * ty + core_at[c]]
                if (dx, dy, c) == (0, 0, 0):
                    post(src, abuf.at[r, q], a_sem.at[0], a_sem.at[1], *to)
                else:
                    push(src, abuf.at[r, q], a_sem.at[0], a_sem.at[1], to)
        return carry

    lax.fori_loop(0, 4, send_ab, 0)

    wait(prow, pair_sem.at[1])

    def tri_gate(s, carry):
        v = prow[s].reshape(HALF, C).astype(F32)
        tg[s] = sigmoid(dot(layer_norm(v).astype(BF16), tri_gate_ref[...]))
        return carry

    lax.fori_loop(0, OWN, tri_gate, 0)

    wait(abuf, a_sem.at[1])
    top = lax.rem(lax.broadcasted_iota(jnp.int32, (1, 16, 128), 1), 8) < 4
    for side in range(2):
        for u in range(4):
            even = abuf[:, 2 * u, side].reshape(256, 128)
            odd = abuf[:, 2 * u + 1, side].reshape(256, 128)
            low = jnp.concatenate([even[:, :64], odd[:, :64]], axis=1)
            high = jnp.concatenate([even[:, 64:], odd[:, 64:]], axis=1)
            if side == 1:
                tiles = [low.reshape(16, 1, 16, 128), high.reshape(16, 1, 16, 128)]
            else:
                tiles = []
                for half in (low, high):
                    half = half.astype(F32).reshape(8, 2, 16, 128)
                    one, two = half[:, 0], half[:, 1]
                    tiles.append(jnp.where(top, one, two).astype(BF16).reshape(8, 1, 16, 128))
                    tiles.append(jnp.where(top, two, one).astype(BF16).reshape(8, 1, 16, 128))
            amat[side, :, 128 * u : 128 * (u + 1)] = jnp.concatenate(tiles, axis=1).reshape(512, 128)

    def product(g, carry):
        x = dot_t(amat[0, pl.ds(pl.multiple_of(128 * g, 128), 128)], amat[1]).reshape(2, 8, 8, 512)
        for mm in range(2):
            for c in range(2):
                tiles = [x[mm, :, :, 128 * t : 128 * (t + 1)] for t in (2 * c, 2 * c + 1)]
                xmsg[4 * g + 2 * mm + c] = jnp.concatenate(tiles, axis=1).astype(BF16)
        return carry

    lax.fori_loop(0, 4, product, 0)
    pltpu.make_async_copy(xmsg.at[r, q], xbuf.at[channel], x_sem.at[1]).start()
    for dx, dy, dz, c in far_first([0, 1]):
        if (dx, dy, dz, c) != (0, 0, 0, 0):
            to = device(xs_at[dx], ys_at[dy], zs_at[dz], core_at[c])
            push(xmsg.at[to[0], to[1]], xbuf.at[channel], x_sem.at[0], x_sem.at[1], to)

    wait(xbuf, x_sem.at[1])
    xs[...] = layer_norm(xbuf[...].astype(F32), 0).reshape(2048, 128)
    for p in range(16):
        s, t = p % 8, p // 8
        xn = xs[pl.ds(p, 128, stride=16)].T.astype(BF16)
        update = dot(xn, tri_out_ref[...])
        v = prow[s, 2 * t : 2 * t + 2].reshape(128, C).astype(F32)
        first = (v + tg[s, 128 * t : 128 * (t + 1)] * update).astype(BF16)
        z1[s, 128 * t : 128 * (t + 1)] = first
        yn[core, s, 128 * t : 128 * (t + 1)] = layer_norm(first.astype(F32)).astype(BF16)

    share = pltpu.make_async_remote_copy(
        src_ref=yn.at[core], dst_ref=yn.at[core], send_sem=yn_sem.at[0], recv_sem=yn_sem.at[1],
        device_id=(r + 1 - 2 * core, q), device_id_type=MESH,
    )
    share.start()

    row_id = lax.broadcasted_iota(jnp.int32, (32, C), 0)
    slot_id = 4 * (row_id // 16) + lax.rem(row_id, 4)
    head_id = lax.rem(row_id // 4, 4)
    columns = jnp.zeros((32, C), F32)
    for h in range(HEADS):
        columns = jnp.where(head_id == h, abias_ref[h : h + 1, :].astype(F32), columns)
    bias = jnp.zeros((32, HALF), F32)
    for s in range(OWN):
        weights = jnp.where(slot_id == s, columns, 0.0).astype(BF16)
        bias += dot_t(weights, yn[core, s])
    bmsg[...] = bias.astype(BF16).reshape(2, 16, HALF)

    def send_bias(block):
        src = bmsg.at[lax.rem(block + flip, 2)]
        dst = bbuf.at[block, core, lax.rem(chip, N_CHIP // 2)]
        for dx, dy, dz, _ in far_first([0]):
            to = device(xs_at[dx], ys_at[dy], zs_at[dz], part)
            if (dx, dy, dz) == (0, 0, 0):
                post(src, dst, b_send.at[block], b_recv.at[block], *to)
            else:
                push(src, dst, b_send.at[block], b_recv.at[block], to)

    def bias_sent(block):
        own_bias = core == part

        @pl.when(own_bias)
        def _():
            wait(bbuf.at[block, 0], b_send.at[block])
            wait(bbuf.at[block, 1, pl.ds(0, 31)], b_send.at[block])

        @pl.when(jnp.logical_not(own_bias))
        def _():
            wait(bbuf.at[block], b_send.at[block])

    send_bias(0)

    sub_id = lax.broadcasted_iota(jnp.int32, (128, C), 0)
    upper = lax.rem(sub_id, 8) < 4
    lane_head = lax.broadcasted_iota(jnp.int32, (2, 8, C), 2) // DH
    row_head = 2 * lax.broadcasted_iota(jnp.int32, (2, 8, C), 0) + (
        lax.broadcasted_iota(jnp.int32, (2, 8, C), 1) // 4
    )
    head_mask = jnp.where(lane_head == row_head, 1.0, 0.0).astype(F32)

    def own_qkvg(s, carry):
        qkvg = dot(yn[core, s], qkvg_ref[...])
        query = (qkvg[:, :C] * DH ** (-0.5)).reshape(4, 2, 32, C)
        for block in range(2):
            v = query[:, block].reshape(128, C)
            down, up = pltpu.roll(v, 4, 0), pltpu.roll(v, 124, 0)
            even = jnp.where(upper, v, down).reshape(16, 1, 1, 8, C)
            odd = jnp.where(upper, up, v).reshape(16, 1, 1, 8, C)
            rows = jnp.concatenate([even * head_mask, odd * head_mask], axis=1)
            qx[block, s] = rows.reshape(512, C).astype(BF16)
        kb[core, s] = qkvg[:, C : 2 * C].astype(BF16)
        vb[core, s] = qkvg[:, 2 * C : 3 * C].astype(BF16)
        ag[s] = sigmoid(qkvg[:, 3 * C :])
        return carry

    lax.fori_loop(0, OWN, own_qkvg, 0)
    share.wait()

    def other_kv(s, carry):
        kv = dot(yn[1 - core, s], qkvg_ref[:, C : 3 * C])
        kb[1 - core, s] = kv[:, :C].astype(BF16)
        vb[1 - core, s] = kv[:, C:].astype(BF16)
        return carry

    lax.fori_loop(0, OWN, other_kv, 0)
    bias_sent(0)
    send_bias(1)

    key_id = lax.broadcasted_iota(jnp.int32, (1, 2 * HALF), 1)
    key_bias = jnp.where(key_id < limit, 0.0, -1000000000.0).astype(F32)

    def attend(block, s):
        keys = kb[:, s].reshape(2 * HALF, C)
        vals = vb[:, s].reshape(2 * HALF, C)
        bias = jnp.concatenate([bbuf[block, 0], bbuf[block, 1]], axis=-1)
        scores = dot_t(qx[block, s], keys) + (bias.reshape(512, 2 * HALF).astype(F32) + key_bias)
        expo = jnp.exp(scores - jnp.max(scores, axis=-1, keepdims=True))
        total = jnp.sum(expo, axis=-1, keepdims=True)
        got = (dot(expo.astype(BF16), vals) / total).reshape(16, 2, 2, 8, C) * head_mask
        got = jnp.sum(got, axis=2)
        even, odd = got[:, 0].reshape(128, C), got[:, 1].reshape(128, C)
        even = even + pltpu.roll(even, 124, 0)
        odd = odd + pltpu.roll(odd, 4, 0)
        return jnp.where(upper, even, odd)

    for block in range(2):
        wait(bbuf.at[block], b_recv.at[block])

        def finish(s, carry, block=block):
            gate = ag[s].reshape(4, 2, 32, C)[:, block].reshape(128, C)
            first = z1[s].reshape(4, 2, 32, C)[:, block].reshape(128, C)
            gated = (gate * attend(block, s)).astype(BF16)
            done = first.astype(F32) + dot(gated, aout_ref[...])
            omsg[s, :, 32 * block : 32 * (block + 1)] = done.astype(BF16).reshape(4, 32, C)
            side = lax.rem(s // 4 + flip, 2)
            for u in range(4):
                src = omsg.at[s, u, pl.ds(32 * block, 32)]
                dst = out_ref.at[4 * q + lax.rem(s, 4), pl.ds(32 * block, 32)]
                post(src, dst, o_sem.at[0], o_sem.at[1], 2 * (r // 2) + side, 4 * core + u)
            return carry

        lax.fori_loop(0, OWN, finish, 0)

    wait(amsg.at[pl.ds(0, N_DEV - 1)], a_sem.at[0])
    wait(xbuf.at[pl.ds(0, N_DEV - 1)], x_sem.at[0])
    own_block = core == q // 4
    @pl.when(own_block)
    def _():
        wait(prow.at[pl.ds(0, 7)], pair_sem.at[0])
        wait(prow.at[pl.ds(0, 7)], o_sem.at[0])

    @pl.when(jnp.logical_not(own_block))
    def _():
        wait(prow, pair_sem.at[0])
        wait(prow, o_sem.at[0])

    bias_sent(1)
    wait(out_ref, o_sem.at[1])


def local(pair, valid_len, tri_in, tri_gate, tri_out, att_qkvg, att_bias, att_out):
    hbm = pl.BlockSpec(memory_space=pltpu.HBM)
    smem = pl.BlockSpec(memory_space=pltpu.SMEM)
    dma = pltpu.SemaphoreType.DMA
    return pl.pallas_call(
        kernel,
        out_shape=jax.ShapeDtypeStruct(pair.shape, pair.dtype),
        in_specs=[hbm, smem] + [hbm] * 6,
        out_specs=hbm,
        scratch_shapes=[
            pltpu.VMEM(tri_in.shape, BF16),
            pltpu.VMEM(tri_gate.shape, BF16),
            pltpu.VMEM(tri_out.shape, BF16),
            pltpu.VMEM(att_qkvg.shape, BF16),
            pltpu.VMEM(att_bias.shape[::-1], BF16),
            pltpu.VMEM(att_out.shape, BF16),
            pltpu.VMEM((ROWS, COLS, C), BF16),
            pltpu.VMEM((16, 2, COLS, C), BF16),
            pltpu.VMEM((4 * C, C), BF16),
            pltpu.VMEM((1024, 128), F32),
            pltpu.VMEM((N_DEV, 2, 16, 128), BF16),
            pltpu.VMEM((N_ROW, N_COL, 2, 16, 128), BF16),
            pltpu.VMEM((2, 512, 512), BF16),
            pltpu.VMEM((N_ROW, N_COL, 16, 128), BF16),
            pltpu.VMEM((N_DEV, 16, 128), BF16),
            pltpu.VMEM((2048, 128), F32),
            pltpu.VMEM((OWN, 4, COLS, C), BF16),
            pltpu.VMEM((OWN, HALF, C), F32),
            pltpu.VMEM((OWN, HALF, C), BF16),
            pltpu.VMEM((2, OWN, HALF, C), BF16),
            pltpu.VMEM((2, 16, HALF), BF16),
            pltpu.VMEM((2, 2, N_CHIP // 2, 16, HALF), BF16),
            pltpu.VMEM((2, OWN, 512, C), BF16),
            pltpu.VMEM((2, OWN, HALF, C), BF16),
            pltpu.VMEM((2, OWN, HALF, C), BF16),
            pltpu.VMEM((OWN, HALF, C), F32),
            pltpu.VMEM((OWN, 4, COLS, C), BF16),
            dma((7,)),
            pltpu.SemaphoreType.REGULAR,
            dma((2,)),
            dma((2,)),
            dma((2,)),
            dma((2,)),
            dma((2,)),
            dma((2,)),
            dma((2,)),
        ],
        compiler_params=pltpu.CompilerParams(
            collective_id=0, has_side_effects=True, vmem_limit_bytes=63 * 2**20
        ),
        name="pairformer",
    )(pair, valid_len, tri_in, tri_gate, tri_out, att_qkvg, att_bias.T, att_out)


def solution(mesh):
    placed = (P("row", "col", None), P(), P(), P(), P(), P(), P(), P())
    return jax.shard_map(
        local, mesh=mesh, in_specs=placed, out_specs=P("row", "col", None), check_vma=False
    )
```

```python
import itertools

import jax
import jax.numpy as jnp
from jax import lax
from jax.experimental import pallas as pl
from jax.experimental.pallas import tpu as pltpu
from jax.sharding import PartitionSpec as P

MESH = pl.DeviceIdType.MESH
BF16, F32 = jnp.bfloat16, jnp.float32
N_ROW, N_COL, N_DEV, N_CHIP = 16, 8, 128, 64
ROWS, COLS, OWN, HALF, C = 32, 64, 8, 256, 128
HEADS, DH = 4, 32


def layer_norm(values, axis=-1):
    mean = jnp.mean(values, axis=axis, keepdims=True)
    centred = values - mean
    var = jnp.mean(centred * centred, axis=axis, keepdims=True)
    return centred * lax.rsqrt(var + 1e-05)


def sigmoid(values):
    return 0.5 * jnp.tanh(0.5 * values) + 0.5


def dot(a, b):
    return jnp.dot(a, b, preferred_element_type=F32)


def dot_t(a, b):
    return lax.dot_general(a, b, (((1,), (1,)), ((), ())), preferred_element_type=F32)


def far_first(cores):
    ring = (0, 1, 2, 1)
    steps = itertools.product(range(4), range(4), range(4), cores)
    return sorted(steps, key=lambda d: -(ring[d[0]] + ring[d[1]] + ring[d[2]]))


def wait(ref, sem):
    pltpu.make_async_copy(ref, ref, sem).wait()


def kernel(
    pair_ref, limit_ref, tri_in_hbm, tri_gate_hbm, tri_out_hbm, qkvg_hbm, abias_hbm, aout_hbm,
    out_ref,
    tri_in_ref, tri_gate_ref, tri_out_ref, qkvg_ref, abias_ref, aout_ref,
    pair_v, zn, wt, stage, amsg, abuf, amat, xmsg, xbuf, xs, prow, tg, z1, yn, bmsg, bbuf,
    qx, kb, vb, ag, omsg, full_bias, raw,
    load_sem, in_sem, pair_sem, a_sem, x_sem, yn_sem, b_send, b_recv, o_sem,
):
    r, q = lax.axis_index("row"), lax.axis_index("col")
    me = r * N_COL + q
    core = lax.rem(r, 2)
    chip = (r // 2) * N_COL + q
    part = chip // (N_CHIP // 2)
    limit = limit_ref[0]
    flip = lax.rem(q, 4) // 2

    cx, cy, cz = 2 * (q // 4) + r // 8, lax.rem(q, 4), lax.rem(r // 2, 4)
    xs_at = [lax.rem(cx + d, 4) for d in range(4)]
    ys_at = [lax.rem(cy + d, 4) for d in range(4)]
    zs_at = [lax.rem(cz + d, 4) for d in range(4)]
    core_at = [core, 1 - core]
    quarter = lax.rem(cx + cy + cz, 4)
    channel = 32 * quarter + 8 * cx + 2 * cy + core

    def device(x, y, z, which):
        return 8 * lax.rem(x, 2) + 2 * z + which, 4 * (x // 2) + y

    def push(src, dst, send, recv, to):
        pltpu.make_async_remote_copy(
            src_ref=src, dst_ref=dst, send_sem=send, recv_sem=recv,
            device_id=to, device_id_type=MESH,
        ).start()

    def at(device):
        return (device // N_COL, lax.rem(device, N_COL))

    def post(src, dst, send, recv, row, col):
        here = jnp.logical_and(row == r, col == q)

        @pl.when(here)
        def _():
            pltpu.make_async_copy(src, dst, recv).start()

        @pl.when(jnp.logical_not(here))
        def _():
            pltpu.make_async_remote_copy(
                src_ref=src, dst_ref=dst, send_sem=send, recv_sem=recv,
                device_id=(row, col), device_id_type=MESH,
            ).start()

    loads = [
        pltpu.make_async_copy(src, dst, load_sem.at[k])
        for k, (src, dst) in enumerate(
            [
                (pair_ref, pair_v), (tri_in_hbm, tri_in_ref), (tri_gate_hbm, tri_gate_ref),
                (tri_out_hbm, tri_out_ref), (qkvg_hbm, qkvg_ref), (abias_hbm, abias_ref),
                (aout_hbm, aout_ref),
            ]
        )
    ]
    for load in loads:
        load.start()
    barrier = pltpu.get_barrier_semaphore()
    mates = [(2 * (r // 2) + core_at[c], lax.rem(q + k, N_COL)) for c in range(2) for k in range(N_COL)]
    peers = [(lax.rem(r + 2 * k, N_ROW), q) for k in range(1, N_ROW // 2)]
    for to in mates[1:] + peers:
        pl.semaphore_signal(barrier, inc=1, device_id=to, device_id_type=MESH)
    for load in loads:
        load.wait()
    pl.semaphore_wait(barrier, len(mates) - 1 + len(peers))
    for to in peers:
        pl.semaphore_signal(in_sem, inc=1, device_id=to, device_id_type=MESH)
    for k in (6, 2, 5, 7, 3, 1, 4, 0):
        col = lax.rem(q + k, N_COL)
        slot = 4 * lax.rem(core + lax.rem(col, 4) // 2, 2)
        src = pair_v.at[pl.ds(4 * col, 4)]
        dst = prow.at[pl.ds(slot, 4), lax.rem(q, 4)]
        post(src, dst, pair_sem.at[0], pair_sem.at[1], 2 * (r // 2) + q // 4, col)

    wt[...] = tri_in_ref[...].T

    def norm_block(b, carry):
        v = pair_v[pl.ds(4 * b, 4)].astype(F32)
        zn[pl.ds(4 * lax.rem(b, 4), 4), b // 4] = layer_norm(v).astype(BF16)
        return carry

    lax.fori_loop(0, 8, norm_block, 0)
    pl.semaphore_wait(in_sem, len(peers))

    s_id = lax.broadcasted_iota(jnp.int32, (16, 128), 0)
    l_id = lax.broadcasted_iota(jnp.int32, (16, 128), 1)
    k_id = COLS * q + lax.rem(l_id, COLS)
    quad = s_id // 4 + core * (1 - 2 * lax.rem(s_id // 4, 2))
    quad = 2 * lax.rem(quad, 2) + quad // 2

    def masked(s_order):
        i_id = ROWS * r + 16 * (l_id // COLS) + s_order
        return jnp.where((i_id < limit) & (k_id < limit), 1.0, 0.0).astype(F32)

    mask = jnp.stack([masked(4 * quad + lax.rem(s_id, 4)), masked(s_id)])

    planes = sorted(itertools.product(range(4), range(4)), key=lambda d: -(d[0] % 2 + d[1] % 2))

    def send_ab(n, carry):
        ahead = lax.rem(n + 1, 4)
        group = lax.rem(quarter + ahead, 4)
        first = 32 * group
        weights = jnp.concatenate(
            [wt[pl.ds(pl.multiple_of(k * C + first, 32), 32)] for k in range(4)], axis=0
        )

        def gate(piece, inner):
            rhs = zn[pl.ds(4 * piece, 4)].reshape(512, C)
            proj = dot_t(weights, rhs)
            a = sigmoid(proj[0:32]) * proj[32:64]
            b = sigmoid(proj[64:96]) * proj[96:128]
            swapped = 2 * lax.rem(piece, 2) + piece // 2
            place = 4 * (swapped + core * (1 - 2 * lax.rem(swapped, 2)))
            for k in range(4):
                stage[pl.ds(place + k, 32, stride=32)] = a[:, 128 * k : 128 * (k + 1)]
                stage[pl.ds(16 + 4 * piece + k, 32, stride=32)] = b[:, 128 * k : 128 * (k + 1)]
            return inner

        lax.fori_loop(0, 4, gate, 0)
        both = stage[...].reshape(32, 2, 16, 128) * mask
        amsg[pl.ds(first, 32)] = both.astype(BF16)

        for dx, dy in planes:
            tx, ty = xs_at[dx], ys_at[dy]
            tz = lax.rem(group + 8 - tx - ty, 4)
            for c in range(2):
                to = device(tx, ty, tz, core_at[c])
                src = amsg.at[first + 8 * tx + 2 * ty + core_at[c]]
                if (dx, dy, c) == (0, 0, 0):
                    post(src, abuf.at[r, q], a_sem.at[0], a_sem.at[1], *to)
                else:
                    push(src, abuf.at[r, q], a_sem.at[0], a_sem.at[1], to)
        return carry

    lax.fori_loop(0, 4, send_ab, 0)

    wait(prow, pair_sem.at[1])

    def tri_gate(s, carry):
        v = prow[s].reshape(HALF, C).astype(F32)
        tg[s] = sigmoid(dot(layer_norm(v).astype(BF16), tri_gate_ref[...]))
        return carry

    lax.fori_loop(0, OWN, tri_gate, 0)

    wait(abuf, a_sem.at[1])
    top = lax.rem(lax.broadcasted_iota(jnp.int32, (1, 16, 128), 1), 8) < 4
    for side in range(2):
        for u in range(4):
            even = abuf[:, 2 * u, side].reshape(256, 128)
            odd = abuf[:, 2 * u + 1, side].reshape(256, 128)
            low = jnp.concatenate([even[:, :64], odd[:, :64]], axis=1)
            high = jnp.concatenate([even[:, 64:], odd[:, 64:]], axis=1)
            if side == 1:
                tiles = [low.reshape(16, 1, 16, 128), high.reshape(16, 1, 16, 128)]
            else:
                tiles = []
                for half in (low, high):
                    half = half.astype(F32).reshape(8, 2, 16, 128)
                    one, two = half[:, 0], half[:, 1]
                    tiles.append(jnp.where(top, one, two).astype(BF16).reshape(8, 1, 16, 128))
                    tiles.append(jnp.where(top, two, one).astype(BF16).reshape(8, 1, 16, 128))
            amat[side, :, 128 * u : 128 * (u + 1)] = jnp.concatenate(tiles, axis=1).reshape(512, 128)

    x = dot_t(amat[0], amat[1]).reshape(8, 8, 8, 512)
    for m in range(8):
        for c in range(2):
            tiles = [x[m, :, :, 128 * t : 128 * (t + 1)] for t in (2 * c, 2 * c + 1)]
            xmsg[2 * m + c] = jnp.concatenate(tiles, axis=1).astype(BF16)

    pltpu.make_async_copy(xmsg.at[r, q], xbuf.at[channel], x_sem.at[1]).start()
    for dx, dy, dz, c in far_first([0, 1]):
        if (dx, dy, dz, c) != (0, 0, 0, 0):
            to = device(xs_at[dx], ys_at[dy], zs_at[dz], core_at[c])
            push(xmsg.at[to[0], to[1]], xbuf.at[channel], x_sem.at[0], x_sem.at[1], to)

    wait(xbuf, x_sem.at[1])
    xs[...] = layer_norm(xbuf[...].astype(F32), 0).reshape(2048, 128)
    row_id = lax.broadcasted_iota(jnp.int32, (16, C), 0)
    columns = jnp.zeros((16, C), F32)
    for h in range(HEADS):
        columns = jnp.where(row_id // 4 == h, abias_ref[h : h + 1, :].astype(F32), columns)
    x_hi = cx // 2

    def spread(block):
        dst = bbuf.at[block, :, core, cz, x_hi, cy]
        for dx, dy, dz, _ in far_first([0]):
            to = device(xs_at[dx], ys_at[dy], zs_at[dz], part)
            if (dx, dy, dz) == (0, 0, 0):
                post(bmsg.at[block], dst, b_send.at[block], b_recv.at[block], *to)
            else:
                push(bmsg.at[block], dst, b_send.at[block], b_recv.at[block], to)

    def spread_done(block):
        @pl.when(core == part)
        def _():
            wait(bbuf.at[block, :, 0], b_send.at[block])
            wait(bbuf.at[block, :, 1, pl.ds(0, 3)], b_send.at[block])
            wait(bbuf.at[block, :, 1, 0, 0, pl.ds(0, 3)], b_send.at[block])
            wait(bbuf.at[block, :, 1, 0, 1], b_send.at[block])

        @pl.when(core != part)
        def _():
            wait(bbuf.at[block], b_send.at[block])

    for block in range(2):
        group = 4 * lax.rem(flip + block, 2)
        bias = jnp.zeros((16, HALF), F32)
        for k in range(4):
            slot = group + k
            normed = []
            for t in range(2):
                xn = xs[pl.ds(8 * t + slot, 128, stride=16)].T.astype(BF16)
                update = dot(xn, tri_out_ref[...])
                v = prow[slot, 2 * t : 2 * t + 2].reshape(128, C).astype(F32)
                first = (v + tg[slot, 128 * t : 128 * (t + 1)] * update).astype(BF16)
                z1[slot, 128 * t : 128 * (t + 1)] = first
                normed.append(layer_norm(first.astype(F32)).astype(BF16))
            normed = jnp.concatenate(normed, axis=0)
            yn[core, slot] = normed
            weights = jnp.where(lax.rem(row_id, 4) == k, columns, 0.0).astype(BF16)
            bias += dot_t(weights, normed)
        for t in range(2):
            bmsg[block, t] = bias[:, 128 * t : 128 * (t + 1)].astype(BF16)
        if block == 0:
            spread(0)
        rows = yn.at[core, pl.ds(group, 4)]
        push(rows, rows, yn_sem.at[0], yn_sem.at[1], (r + 1 - 2 * core, q))

    sub_id = lax.broadcasted_iota(jnp.int32, (128, C), 0)
    upper = lax.rem(sub_id, 8) < 4
    lane_head = lax.broadcasted_iota(jnp.int32, (2, 8, C), 2) // DH
    row_head = 2 * lax.broadcasted_iota(jnp.int32, (2, 8, C), 0) + (
        lax.broadcasted_iota(jnp.int32, (2, 8, C), 1) // 4
    )
    head_mask = jnp.where(lane_head == row_head, 1.0, 0.0).astype(F32)

    def own_qkvg(s, carry):
        qkvg = dot(yn[core, s], qkvg_ref[...])
        query = (qkvg[:, :C] * DH ** (-0.5)).reshape(4, 2, 32, C)
        for block in range(2):
            v = query[:, block].reshape(128, C)
            down, up = pltpu.roll(v, 4, 0), pltpu.roll(v, 124, 0)
            even = jnp.where(upper, v, down).reshape(16, 1, 1, 8, C)
            odd = jnp.where(upper, up, v).reshape(16, 1, 1, 8, C)
            rows = jnp.concatenate([even * head_mask, odd * head_mask], axis=1)
            qx[block, s] = rows.reshape(512, C).astype(BF16)
        kb[core, s] = qkvg[:, C : 2 * C].astype(BF16)
        vb[core, s] = qkvg[:, 2 * C : 3 * C].astype(BF16)
        ag[s] = sigmoid(qkvg[:, 3 * C :])
        return carry

    lax.fori_loop(0, OWN, own_qkvg, 0)
    wait(yn.at[0], yn_sem.at[1])

    def other_kv(s, carry):
        kv = dot(yn[1 - core, s], qkvg_ref[:, C : 3 * C])
        kb[1 - core, s] = kv[:, :C].astype(BF16)
        vb[1 - core, s] = kv[:, C:].astype(BF16)
        return carry

    lax.fori_loop(0, OWN, other_kv, 0)

    def multiply(block):
        def one(s, carry):
            raw[block, s] = dot_t(qx[block, s], kb[:, s].reshape(2 * HALF, C))
            return carry

        lax.fori_loop(0, OWN, one, 0)

    multiply(0)
    spread_done(0)
    spread(1)
    multiply(1)

    key_id = lax.broadcasted_iota(jnp.int32, (1, 2 * HALF), 1)
    key_bias = jnp.where(key_id < limit, 0.0, -1000000000.0).astype(F32)

    def attend(block, s):
        vals = vb[:, s].reshape(2 * HALF, C)
        scores = raw[block, s] + full_bias[...]
        expo = jnp.exp(scores - jnp.max(scores, axis=-1, keepdims=True))
        total = jnp.sum(expo, axis=-1, keepdims=True)
        got = (dot(expo.astype(BF16), vals) / total).reshape(16, 2, 2, 8, C) * head_mask
        got = jnp.sum(got, axis=2)
        even, odd = got[:, 0].reshape(128, C), got[:, 1].reshape(128, C)
        even = even + pltpu.roll(even, 124, 0)
        odd = odd + pltpu.roll(odd, 4, 0)
        return jnp.where(upper, even, odd)

    for block in range(2):
        wait(bbuf.at[block], b_recv.at[block])
        tiles = [bbuf[block, t, c].reshape(512, 128) for c in range(2) for t in range(2)]
        full_bias[...] = jnp.concatenate(tiles, axis=-1).astype(F32) + key_bias

        def finish(s, carry, block=block):
            gate = ag[s].reshape(4, 2, 32, C)[:, block].reshape(128, C)
            first = z1[s].reshape(4, 2, 32, C)[:, block].reshape(128, C)
            gated = (gate * attend(block, s)).astype(BF16)
            done = first.astype(F32) + dot(gated, aout_ref[...])
            omsg[s, :, 32 * block : 32 * (block + 1)] = done.astype(BF16).reshape(4, 32, C)
            side = lax.rem(s // 4 + flip, 2)
            for u in range(4):
                src = omsg.at[s, u, pl.ds(32 * block, 32)]
                dst = out_ref.at[4 * q + lax.rem(s, 4), pl.ds(32 * block, 32)]
                post(src, dst, o_sem.at[0], o_sem.at[1], 2 * (r // 2) + side, 4 * core + u)
            return carry

        lax.fori_loop(0, OWN, finish, 0)

    wait(amsg.at[pl.ds(0, N_DEV - 1)], a_sem.at[0])
    wait(xbuf.at[pl.ds(0, N_DEV - 1)], x_sem.at[0])
    own_block = core == q // 4
    @pl.when(own_block)
    def _():
        wait(prow.at[pl.ds(0, 7)], pair_sem.at[0])
        wait(prow.at[pl.ds(0, 7)], o_sem.at[0])

    @pl.when(jnp.logical_not(own_block))
    def _():
        wait(prow, pair_sem.at[0])
        wait(prow, o_sem.at[0])

    wait(yn.at[0], yn_sem.at[0])
    spread_done(1)
    wait(out_ref, o_sem.at[1])


def local(pair, valid_len, tri_in, tri_gate, tri_out, att_qkvg, att_bias, att_out):
    hbm = pl.BlockSpec(memory_space=pltpu.HBM)
    smem = pl.BlockSpec(memory_space=pltpu.SMEM)
    dma = pltpu.SemaphoreType.DMA
    return pl.pallas_call(
        kernel,
        out_shape=jax.ShapeDtypeStruct(pair.shape, pair.dtype),
        in_specs=[hbm, smem] + [hbm] * 6,
        out_specs=hbm,
        scratch_shapes=[
            pltpu.VMEM(tri_in.shape, BF16),
            pltpu.VMEM(tri_gate.shape, BF16),
            pltpu.VMEM(tri_out.shape, BF16),
            pltpu.VMEM(att_qkvg.shape, BF16),
            pltpu.VMEM(att_bias.shape[::-1], BF16),
            pltpu.VMEM(att_out.shape, BF16),
            pltpu.VMEM((ROWS, COLS, C), BF16),
            pltpu.VMEM((16, 2, COLS, C), BF16),
            pltpu.VMEM((4 * C, C), BF16),
            pltpu.VMEM((1024, 128), F32),
            pltpu.VMEM((N_DEV, 2, 16, 128), BF16),
            pltpu.VMEM((N_ROW, N_COL, 2, 16, 128), BF16),
            pltpu.VMEM((2, 512, 512), BF16),
            pltpu.VMEM((N_ROW, N_COL, 16, 128), BF16),
            pltpu.VMEM((N_DEV, 16, 128), BF16),
            pltpu.VMEM((2048, 128), F32),
            pltpu.VMEM((OWN, 4, COLS, C), BF16),
            pltpu.VMEM((OWN, HALF, C), F32),
            pltpu.VMEM((OWN, HALF, C), BF16),
            pltpu.VMEM((2, OWN, HALF, C), BF16),
            pltpu.VMEM((2, 2, 16, 128), BF16),
            pltpu.VMEM((2, 2, 2, 4, 2, 4, 16, 128), BF16),
            pltpu.VMEM((2, OWN, 512, C), BF16),
            pltpu.VMEM((2, OWN, HALF, C), BF16),
            pltpu.VMEM((2, OWN, HALF, C), BF16),
            pltpu.VMEM((OWN, HALF, C), F32),
            pltpu.VMEM((OWN, 4, COLS, C), BF16),
            pltpu.VMEM((512, 2 * HALF), F32),
            pltpu.VMEM((2, OWN, 512, 2 * HALF), F32),
            dma((7,)),
            pltpu.SemaphoreType.REGULAR,
            dma((2,)),
            dma((2,)),
            dma((2,)),
            dma((2,)),
            dma((2,)),
            dma((2,)),
            dma((2,)),
        ],
        compiler_params=pltpu.CompilerParams(
            collective_id=0, has_side_effects=True, vmem_limit_bytes=63 * 2**20
        ),
        name="pairformer",
    )(pair, valid_len, tri_in, tri_gate, tri_out, att_qkvg, att_bias.T, att_out)


def solution(mesh):
    placed = (P("row", "col", None), P(), P(), P(), P(), P(), P(), P())
    return jax.shard_map(
        local, mesh=mesh, in_specs=placed, out_specs=P("row", "col", None), check_vma=False
    )
```

```python
import itertools

import jax
import jax.numpy as jnp
from jax import lax
from jax.experimental import pallas as pl
from jax.experimental.pallas import tpu as pltpu
from jax.sharding import PartitionSpec as P

MESH = pl.DeviceIdType.MESH
BF16, F32 = jnp.bfloat16, jnp.float32
N_ROW, N_COL, N_DEV, N_CHIP = 16, 8, 128, 64
ROWS, COLS, OWN, HALF, C = 32, 64, 8, 256, 128
HEADS, DH = 4, 32


def layer_norm(values, axis=-1):
    mean = jnp.mean(values, axis=axis, keepdims=True)
    centred = values - mean
    var = jnp.mean(centred * centred, axis=axis, keepdims=True)
    return centred * lax.rsqrt(var + 1e-05)


def sigmoid(values):
    return 0.5 * jnp.tanh(0.5 * values) + 0.5


def dot(a, b):
    return jnp.dot(a, b, preferred_element_type=F32)


def dot_t(a, b):
    return lax.dot_general(a, b, (((1,), (1,)), ((), ())), preferred_element_type=F32)


def far_first(cores):
    ring = (0, 1, 2, 1)
    steps = itertools.product(range(4), range(4), range(4), cores)
    return sorted(steps, key=lambda d: -(ring[d[0]] + ring[d[1]] + ring[d[2]]))


def wait(ref, sem):
    pltpu.make_async_copy(ref, ref, sem).wait()


def kernel(
    pair_ref, limit_ref, tri_in_hbm, tri_gate_hbm, tri_out_hbm, qkvg_hbm, abias_hbm, aout_hbm,
    out_ref,
    tri_in_ref, tri_gate_ref, tri_out_ref, qkvg_ref, abias_ref, aout_ref,
    pair_v, zn, wt, stage, amsg, abuf, amat, xmsg, xbuf, xs, prow, tg, z1, yn, bmsg, bbuf,
    qx, kb, vb, ag, omsg, full_bias, raw,
    load_sem, in_sem, pair_sem, a_sem, x_sem, yn_sem, b_send, b_recv, o_sem,
):
    r, q = lax.axis_index("row"), lax.axis_index("col")
    me = r * N_COL + q
    core = lax.rem(r, 2)
    chip = (r // 2) * N_COL + q
    part = chip // (N_CHIP // 2)
    limit = limit_ref[0]
    flip = lax.rem(q, 4) // 2

    cx, cy, cz = 2 * (q // 4) + r // 8, lax.rem(q, 4), lax.rem(r // 2, 4)
    xs_at = [lax.rem(cx + d, 4) for d in range(4)]
    ys_at = [lax.rem(cy + d, 4) for d in range(4)]
    zs_at = [lax.rem(cz + d, 4) for d in range(4)]
    core_at = [core, 1 - core]
    quarter = lax.rem(cx + cy + cz, 4)
    channel = 32 * quarter + 8 * cx + 2 * cy + core

    def device(x, y, z, which):
        return 8 * lax.rem(x, 2) + 2 * z + which, 4 * (x // 2) + y

    def push(src, dst, send, recv, to):
        pltpu.make_async_remote_copy(
            src_ref=src, dst_ref=dst, send_sem=send, recv_sem=recv,
            device_id=to, device_id_type=MESH,
        ).start()

    def at(device):
        return (device // N_COL, lax.rem(device, N_COL))

    def post(src, dst, send, recv, row, col):
        here = jnp.logical_and(row == r, col == q)

        @pl.when(here)
        def _():
            pltpu.make_async_copy(src, dst, recv).start()

        @pl.when(jnp.logical_not(here))
        def _():
            pltpu.make_async_remote_copy(
                src_ref=src, dst_ref=dst, send_sem=send, recv_sem=recv,
                device_id=(row, col), device_id_type=MESH,
            ).start()

    loads = [
        pltpu.make_async_copy(src, dst, load_sem.at[k])
        for k, (src, dst) in enumerate(
            [
                (pair_ref, pair_v), (tri_in_hbm, tri_in_ref), (tri_gate_hbm, tri_gate_ref),
                (tri_out_hbm, tri_out_ref), (qkvg_hbm, qkvg_ref), (abias_hbm, abias_ref),
                (aout_hbm, aout_ref),
            ]
        )
    ]
    for load in loads:
        load.start()
    barrier = pltpu.get_barrier_semaphore()
    mates = [(2 * (r // 2) + core_at[c], lax.rem(q + k, N_COL)) for c in range(2) for k in range(N_COL)]
    peers = [(lax.rem(r + 2 * k, N_ROW), q) for k in range(1, N_ROW // 2)]
    for to in mates[1:] + peers:
        pl.semaphore_signal(barrier, inc=1, device_id=to, device_id_type=MESH)
    for load in loads:
        load.wait()
    pl.semaphore_wait(barrier, len(mates) - 1 + len(peers))
    for to in peers:
        pl.semaphore_signal(in_sem, inc=1, device_id=to, device_id_type=MESH)
    for k in (6, 2, 5, 7, 3, 1, 4, 0):
        col = lax.rem(q + k, N_COL)
        slot = 4 * lax.rem(core + lax.rem(col, 4) // 2, 2)
        src = pair_v.at[pl.ds(4 * col, 4)]
        dst = prow.at[pl.ds(slot, 4), lax.rem(q, 4)]
        post(src, dst, pair_sem.at[0], pair_sem.at[1], 2 * (r // 2) + q // 4, col)

    wt[...] = tri_in_ref[...].T

    def norm_block(b, carry):
        v = pair_v[pl.ds(4 * b, 4)].astype(F32)
        zn[pl.ds(4 * lax.rem(b, 4), 4), b // 4] = layer_norm(v).astype(BF16)
        return carry

    lax.fori_loop(0, 8, norm_block, 0)
    pl.semaphore_wait(in_sem, len(peers))

    s_id = lax.broadcasted_iota(jnp.int32, (16, 128), 0)
    l_id = lax.broadcasted_iota(jnp.int32, (16, 128), 1)
    k_id = COLS * q + lax.rem(l_id, COLS)
    quad = s_id // 4 + core * (1 - 2 * lax.rem(s_id // 4, 2))
    quad = 2 * lax.rem(quad, 2) + quad // 2

    def masked(s_order):
        i_id = ROWS * r + 16 * (l_id // COLS) + s_order
        return jnp.where((i_id < limit) & (k_id < limit), 1.0, 0.0).astype(F32)

    mask = jnp.stack([masked(4 * quad + lax.rem(s_id, 4)), masked(s_id)])

    planes = sorted(itertools.product(range(4), range(4)), key=lambda d: -(d[0] % 2 + d[1] % 2))

    def send_ab(n, carry):
        ahead = lax.rem(n + 1, 4)
        group = lax.rem(quarter + ahead, 4)
        first = 32 * group
        weights = jnp.concatenate(
            [wt[pl.ds(pl.multiple_of(k * C + first, 32), 32)] for k in range(4)], axis=0
        )

        def gate(piece, inner):
            rhs = zn[pl.ds(4 * piece, 4)].reshape(512, C)
            proj = dot_t(weights, rhs)
            a = sigmoid(proj[0:32]) * proj[32:64]
            b = sigmoid(proj[64:96]) * proj[96:128]
            swapped = 2 * lax.rem(piece, 2) + piece // 2
            place = 4 * (swapped + core * (1 - 2 * lax.rem(swapped, 2)))
            for k in range(4):
                stage[pl.ds(place + k, 32, stride=32)] = a[:, 128 * k : 128 * (k + 1)]
                stage[pl.ds(16 + 4 * piece + k, 32, stride=32)] = b[:, 128 * k : 128 * (k + 1)]
            return inner

        lax.fori_loop(0, 4, gate, 0)
        both = stage[...].reshape(32, 2, 16, 128) * mask
        amsg[pl.ds(first, 32)] = both.astype(BF16)

        for dx, dy in planes:
            tx, ty = xs_at[dx], ys_at[dy]
            tz = lax.rem(group + 8 - tx - ty, 4)
            for c in range(2):
                to = device(tx, ty, tz, core_at[c])
                src = amsg.at[first + 8 * tx + 2 * ty + core_at[c]]
                if (dx, dy, c) == (0, 0, 0):
                    post(src, abuf.at[r, q], a_sem.at[0], a_sem.at[1], *to)
                else:
                    push(src, abuf.at[r, q], a_sem.at[0], a_sem.at[1], to)
        return carry

    lax.fori_loop(0, 4, send_ab, 0)

    wait(prow, pair_sem.at[1])

    def tri_gate(s, carry):
        v = prow[s].reshape(HALF, C).astype(F32)
        tg[s] = sigmoid(dot(layer_norm(v).astype(BF16), tri_gate_ref[...]))
        return carry

    lax.fori_loop(0, OWN, tri_gate, 0)

    wait(abuf, a_sem.at[1])
    top = lax.rem(lax.broadcasted_iota(jnp.int32, (1, 16, 128), 1), 8) < 4
    for side in range(2):
        for u in range(4):
            even = abuf[:, 2 * u, side].reshape(256, 128)
            odd = abuf[:, 2 * u + 1, side].reshape(256, 128)
            low = jnp.concatenate([even[:, :64], odd[:, :64]], axis=1)
            high = jnp.concatenate([even[:, 64:], odd[:, 64:]], axis=1)
            if side == 1:
                tiles = [low.reshape(16, 1, 16, 128), high.reshape(16, 1, 16, 128)]
            else:
                tiles = []
                for half in (low, high):
                    half = half.astype(F32).reshape(8, 2, 16, 128)
                    one, two = half[:, 0], half[:, 1]
                    tiles.append(jnp.where(top, one, two).astype(BF16).reshape(8, 1, 16, 128))
                    tiles.append(jnp.where(top, two, one).astype(BF16).reshape(8, 1, 16, 128))
            amat[side, :, 128 * u : 128 * (u + 1)] = jnp.concatenate(tiles, axis=1).reshape(512, 128)

    x = dot_t(amat[0], amat[1]).reshape(8, 8, 8, 512)
    for m in range(8):
        for c in range(2):
            tiles = [x[m, :, :, 128 * t : 128 * (t + 1)] for t in (2 * c, 2 * c + 1)]
            xmsg[2 * m + c] = jnp.concatenate(tiles, axis=1).astype(BF16)

    pltpu.make_async_copy(xmsg.at[r, q], xbuf.at[channel], x_sem.at[1]).start()
    for dx, dy, dz, c in far_first([0, 1]):
        if (dx, dy, dz, c) != (0, 0, 0, 0):
            to = device(xs_at[dx], ys_at[dy], zs_at[dz], core_at[c])
            push(xmsg.at[to[0], to[1]], xbuf.at[channel], x_sem.at[0], x_sem.at[1], to)

    wait(xbuf, x_sem.at[1])
    xs[...] = layer_norm(xbuf[...].astype(F32), 0).reshape(2048, 128)
    row_id = lax.broadcasted_iota(jnp.int32, (16, C), 0)
    columns = jnp.zeros((16, C), F32)
    for h in range(HEADS):
        columns = jnp.where(row_id // 4 == h, abias_ref[h : h + 1, :].astype(F32), columns)
    x_hi = cx // 2

    def spread(block):
        dst = bbuf.at[block, :, core, cz, x_hi, cy]
        for dx, dy, dz, _ in far_first([0]):
            to = device(xs_at[dx], ys_at[dy], zs_at[dz], part)
            if (dx, dy, dz) == (0, 0, 0):
                post(bmsg.at[block], dst, b_send.at[block], b_recv.at[block], *to)
            else:
                push(bmsg.at[block], dst, b_send.at[block], b_recv.at[block], to)

    def spread_done(block):
        @pl.when(core == part)
        def _():
            wait(bbuf.at[block, :, 0], b_send.at[block])
            wait(bbuf.at[block, :, 1, pl.ds(0, 3)], b_send.at[block])
            wait(bbuf.at[block, :, 1, 0, 0, pl.ds(0, 3)], b_send.at[block])
            wait(bbuf.at[block, :, 1, 0, 1], b_send.at[block])

        @pl.when(core != part)
        def _():
            wait(bbuf.at[block], b_send.at[block])

    for block in range(2):
        group = 4 * lax.rem(flip + block, 2)
        bias = jnp.zeros((16, HALF), F32)
        for k in range(4):
            slot = group + k
            normed = []
            for t in range(2):
                xn = xs[pl.ds(8 * t + slot, 128, stride=16)].T.astype(BF16)
                update = dot(xn, tri_out_ref[...])
                v = prow[slot, 2 * t : 2 * t + 2].reshape(128, C).astype(F32)
                first = (v + tg[slot, 128 * t : 128 * (t + 1)] * update).astype(BF16)
                z1[slot, 128 * t : 128 * (t + 1)] = first
                normed.append(layer_norm(first.astype(F32)).astype(BF16))
            normed = jnp.concatenate(normed, axis=0)
            yn[core, slot] = normed
            weights = jnp.where(lax.rem(row_id, 4) == k, columns, 0.0).astype(BF16)
            bias += dot_t(weights, normed)
        for t in range(2):
            bmsg[block, t] = bias[:, 128 * t : 128 * (t + 1)].astype(BF16)
        if block == 0:
            spread(0)
        rows = yn.at[core, pl.ds(group, 4)]
        push(rows, rows, yn_sem.at[0], yn_sem.at[1], (r + 1 - 2 * core, q))

    sub_id = lax.broadcasted_iota(jnp.int32, (128, C), 0)
    upper = lax.rem(sub_id, 8) < 4
    lane_head = lax.broadcasted_iota(jnp.int32, (2, 8, C), 2) // DH
    row_head = 2 * lax.broadcasted_iota(jnp.int32, (2, 8, C), 0) + (
        lax.broadcasted_iota(jnp.int32, (2, 8, C), 1) // 4
    )
    head_mask = jnp.where(lane_head == row_head, 1.0, 0.0).astype(F32)

    def own_qkvg(s, carry):
        qkvg = dot(yn[core, s], qkvg_ref[...])
        query = (qkvg[:, :C] * DH ** (-0.5)).reshape(4, 2, 32, C)
        for block in range(2):
            v = query[:, block].reshape(128, C)
            down, up = pltpu.roll(v, 4, 0), pltpu.roll(v, 124, 0)
            even = jnp.where(upper, v, down).reshape(16, 1, 1, 8, C)
            odd = jnp.where(upper, up, v).reshape(16, 1, 1, 8, C)
            rows = jnp.concatenate([even * head_mask, odd * head_mask], axis=1)
            qx[block, s] = rows.reshape(512, C).astype(BF16)
        kb[core, s] = qkvg[:, C : 2 * C].astype(BF16)
        vb[core, s] = qkvg[:, 2 * C : 3 * C].astype(BF16)
        ag[s] = sigmoid(qkvg[:, 3 * C :])
        return carry

    lax.fori_loop(0, OWN, own_qkvg, 0)
    wait(yn.at[0], yn_sem.at[1])

    def other_kv(s, carry):
        kv = dot(yn[1 - core, s], qkvg_ref[:, C : 3 * C])
        kb[1 - core, s] = kv[:, :C].astype(BF16)
        vb[1 - core, s] = kv[:, C:].astype(BF16)
        return carry

    lax.fori_loop(0, OWN, other_kv, 0)

    def multiply(block):
        def one(s, carry):
            raw[block, s] = dot_t(qx[block, s], kb[:, s].reshape(2 * HALF, C))
            return carry

        lax.fori_loop(0, OWN, one, 0)

    multiply(0)
    spread_done(0)
    spread(1)
    multiply(1)

    key_id = lax.broadcasted_iota(jnp.int32, (1, 2 * HALF), 1)
    key_bias = jnp.where(key_id < limit, 0.0, -1000000000.0).astype(F32)

    def attend(block, s):
        vals = vb[:, s].reshape(2 * HALF, C)
        scores = raw[block, s] + full_bias[...]
        expo = jnp.exp(scores - jnp.max(scores, axis=-1, keepdims=True))
        total = jnp.sum(expo, axis=-1, keepdims=True)
        got = (dot(expo.astype(BF16), vals) / total).reshape(16, 2, 2, 8, C) * head_mask
        got = jnp.sum(got, axis=2)
        even, odd = got[:, 0].reshape(128, C), got[:, 1].reshape(128, C)
        even = even + pltpu.roll(even, 124, 0)
        odd = odd + pltpu.roll(odd, 4, 0)
        return jnp.where(upper, even, odd)

    for block in range(2):
        wait(bbuf.at[block], b_recv.at[block])
        tiles = [bbuf[block, t, c].reshape(512, 128) for c in range(2) for t in range(2)]
        full_bias[...] = jnp.concatenate(tiles, axis=-1).astype(F32) + key_bias

        def finish(s, carry, block=block):
            gate = ag[s].reshape(4, 2, 32, C)[:, block].reshape(128, C)
            first = z1[s].reshape(4, 2, 32, C)[:, block].reshape(128, C)
            gated = (gate * attend(block, s)).astype(BF16)
            done = first.astype(F32) + dot(gated, aout_ref[...])
            omsg[s, :, 32 * block : 32 * (block + 1)] = done.astype(BF16).reshape(4, 32, C)
            side = lax.rem(s // 4 + flip, 2)
            for u in range(4):
                src = omsg.at[s, u, pl.ds(32 * block, 32)]
                dst = out_ref.at[4 * q + lax.rem(s, 4), pl.ds(32 * block, 32)]
                post(src, dst, o_sem.at[0], o_sem.at[1], 2 * (r // 2) + side, 4 * core + u)
            return carry

        lax.fori_loop(0, OWN, finish, 0)

    wait(amsg.at[pl.ds(0, N_DEV - 1)], a_sem.at[0])
    wait(xbuf.at[pl.ds(0, N_DEV - 1)], x_sem.at[0])
    own_block = core == q // 4
    @pl.when(own_block)
    def _():
        wait(prow.at[pl.ds(0, 7)], pair_sem.at[0])
        wait(prow.at[pl.ds(0, 7)], o_sem.at[0])

    @pl.when(jnp.logical_not(own_block))
    def _():
        wait(prow, pair_sem.at[0])
        wait(prow, o_sem.at[0])

    wait(yn.at[0], yn_sem.at[0])
    spread_done(1)
    wait(out_ref, o_sem.at[1])


def local(pair, valid_len, tri_in, tri_gate, tri_out, att_qkvg, att_bias, att_out):
    hbm = pl.BlockSpec(memory_space=pl.ANY)

    def hold(array):
        return pltpu.with_memory_space_constraint(array, pltpu.HBM)

    smem = pl.BlockSpec(memory_space=pltpu.SMEM)
    dma = pltpu.SemaphoreType.DMA
    return pl.pallas_call(
        kernel,
        out_shape=jax.ShapeDtypeStruct(pair.shape, pair.dtype),
        in_specs=[hbm, smem] + [hbm] * 6,
        out_specs=hbm,
        scratch_shapes=[
            pltpu.VMEM(tri_in.shape, BF16),
            pltpu.VMEM(tri_gate.shape, BF16),
            pltpu.VMEM(tri_out.shape, BF16),
            pltpu.VMEM(att_qkvg.shape, BF16),
            pltpu.VMEM(att_bias.shape[::-1], BF16),
            pltpu.VMEM(att_out.shape, BF16),
            pltpu.VMEM((ROWS, COLS, C), BF16),
            pltpu.VMEM((16, 2, COLS, C), BF16),
            pltpu.VMEM((4 * C, C), BF16),
            pltpu.VMEM((1024, 128), F32),
            pltpu.VMEM((N_DEV, 2, 16, 128), BF16),
            pltpu.VMEM((N_ROW, N_COL, 2, 16, 128), BF16),
            pltpu.VMEM((2, 512, 512), BF16),
            pltpu.VMEM((N_ROW, N_COL, 16, 128), BF16),
            pltpu.VMEM((N_DEV, 16, 128), BF16),
            pltpu.VMEM((2048, 128), F32),
            pltpu.VMEM((OWN, 4, COLS, C), BF16),
            pltpu.VMEM((OWN, HALF, C), F32),
            pltpu.VMEM((OWN, HALF, C), BF16),
            pltpu.VMEM((2, OWN, HALF, C), BF16),
            pltpu.VMEM((2, 2, 16, 128), BF16),
            pltpu.VMEM((2, 2, 2, 4, 2, 4, 16, 128), BF16),
            pltpu.VMEM((2, OWN, 512, C), BF16),
            pltpu.VMEM((2, OWN, HALF, C), BF16),
            pltpu.VMEM((2, OWN, HALF, C), BF16),
            pltpu.VMEM((OWN, HALF, C), F32),
            pltpu.VMEM((OWN, 4, COLS, C), BF16),
            pltpu.VMEM((512, 2 * HALF), F32),
            pltpu.VMEM((2, OWN, 512, 2 * HALF), F32),
            dma((7,)),
            pltpu.SemaphoreType.REGULAR,
            dma((2,)),
            dma((2,)),
            dma((2,)),
            dma((2,)),
            dma((2,)),
            dma((2,)),
            dma((2,)),
        ],
        compiler_params=pltpu.CompilerParams(
            collective_id=0, has_side_effects=True, vmem_limit_bytes=52 * 2**20
        ),
        name="pairformer",
    )(hold(pair), valid_len, hold(tri_in), hold(tri_gate), hold(tri_out), hold(att_qkvg), hold(att_bias.T), hold(att_out))


def solution(mesh):
    placed = (P("row", "col", None), P(), P(), P(), P(), P(), P(), P())
    return jax.shard_map(
        local, mesh=mesh, in_specs=placed, out_specs=P("row", "col", None), check_vma=False
    )
```

```python
import itertools

import jax
import jax.numpy as jnp
from jax import lax
from jax.experimental import pallas as pl
from jax.experimental.pallas import tpu as pltpu
from jax.sharding import PartitionSpec as P

MESH = pl.DeviceIdType.MESH
BF16, F32 = jnp.bfloat16, jnp.float32
N_ROW, N_COL, N_DEV, N_CHIP = 16, 8, 128, 64
ROWS, COLS, OWN, HALF, C = 32, 64, 8, 256, 128
HEADS, DH = 4, 32


def layer_norm(values, axis=-1):
    mean = jnp.mean(values, axis=axis, keepdims=True)
    centred = values - mean
    var = jnp.mean(centred * centred, axis=axis, keepdims=True)
    return centred * lax.rsqrt(var + 1e-05)


def sigmoid(values):
    return 0.5 * jnp.tanh(0.5 * values) + 0.5


def dot(a, b):
    return jnp.dot(a, b, preferred_element_type=F32)


def dot_t(a, b):
    return lax.dot_general(a, b, (((1,), (1,)), ((), ())), preferred_element_type=F32)


def far_first(cores):
    ring = (0, 1, 2, 1)
    steps = itertools.product(range(4), range(4), range(4), cores)
    return sorted(steps, key=lambda d: -(ring[d[0]] + ring[d[1]] + ring[d[2]]))


def wait(ref, sem):
    pltpu.make_async_copy(ref, ref, sem).wait()


def kernel(
    pair_ref, limit_ref, tri_in_hbm, tri_gate_hbm, tri_out_hbm, qkvg_hbm, abias_hbm, aout_hbm,
    out_ref,
    tri_in_ref, tri_gate_ref, tri_out_ref, qkvg_ref, abias_ref, aout_ref,
    pair_v, zn, wt, stage, amsg, abuf, amat, xmsg, xbuf, xs, prow, tg, z1, yn, bmsg, bbuf,
    qx, kb, vb, ag, omsg, full_bias, raw,
    load_sem, in_sem, pair_sem, a_sem, x_sem, yn_sem, b_send, b_recv, o_sem,
):
    r, q = lax.axis_index("row"), lax.axis_index("col")
    me = r * N_COL + q
    core = lax.rem(r, 2)
    chip = (r // 2) * N_COL + q
    part = chip // (N_CHIP // 2)
    limit = limit_ref[0]
    flip = lax.rem(q, 4) // 2

    cx, cy, cz = 2 * (q // 4) + r // 8, lax.rem(q, 4), lax.rem(r // 2, 4)
    xs_at = [lax.rem(cx + d, 4) for d in range(4)]
    ys_at = [lax.rem(cy + d, 4) for d in range(4)]
    zs_at = [lax.rem(cz + d, 4) for d in range(4)]
    core_at = [core, 1 - core]
    quarter = lax.rem(cx + cy + cz, 4)
    channel = 32 * quarter + 8 * cx + 2 * cy + core

    def device(x, y, z, which):
        return 8 * lax.rem(x, 2) + 2 * z + which, 4 * (x // 2) + y

    def push(src, dst, send, recv, to):
        pltpu.make_async_remote_copy(
            src_ref=src, dst_ref=dst, send_sem=send, recv_sem=recv,
            device_id=to, device_id_type=MESH,
        ).start()

    def at(device):
        return (device // N_COL, lax.rem(device, N_COL))

    def post(src, dst, send, recv, row, col):
        here = jnp.logical_and(row == r, col == q)

        @pl.when(here)
        def _():
            pltpu.make_async_copy(src, dst, recv).start()

        @pl.when(jnp.logical_not(here))
        def _():
            pltpu.make_async_remote_copy(
                src_ref=src, dst_ref=dst, send_sem=send, recv_sem=recv,
                device_id=(row, col), device_id_type=MESH,
            ).start()

    loads = [
        pltpu.make_async_copy(src, dst, load_sem.at[k])
        for k, (src, dst) in enumerate(
            [
                (pair_ref, pair_v), (tri_in_hbm, tri_in_ref), (tri_gate_hbm, tri_gate_ref),
                (tri_out_hbm, tri_out_ref), (qkvg_hbm, qkvg_ref), (abias_hbm, abias_ref),
                (aout_hbm, aout_ref),
            ]
        )
    ]
    for load in loads:
        load.start()
    barrier = pltpu.get_barrier_semaphore()
    mates = [(2 * (r // 2) + core_at[c], lax.rem(q + k, N_COL)) for c in range(2) for k in range(N_COL)]
    peers = [(lax.rem(r + 2 * k, N_ROW), q) for k in range(1, N_ROW // 2)]
    for to in mates[1:] + peers:
        pl.semaphore_signal(barrier, inc=1, device_id=to, device_id_type=MESH)
    for load in loads:
        load.wait()
    pl.semaphore_wait(barrier, len(mates) - 1 + len(peers))
    for to in peers:
        pl.semaphore_signal(in_sem, inc=1, device_id=to, device_id_type=MESH)
    for k in (6, 2, 5, 7, 3, 1, 4, 0):
        col = lax.rem(q + k, N_COL)
        slot = 4 * lax.rem(core + lax.rem(col, 4) // 2, 2)
        src = pair_v.at[pl.ds(4 * col, 4)]
        dst = prow.at[pl.ds(slot, 4), lax.rem(q, 4)]
        post(src, dst, pair_sem.at[0], pair_sem.at[1], 2 * (r // 2) + q // 4, col)

    wt[...] = tri_in_ref[...].T

    def norm_block(b, carry):
        v = pair_v[pl.ds(4 * b, 4)].astype(F32)
        zn[pl.ds(4 * lax.rem(b, 4), 4), b // 4] = layer_norm(v).astype(BF16)
        return carry

    lax.fori_loop(0, 8, norm_block, 0)

    s_id = lax.broadcasted_iota(jnp.int32, (16, 128), 0)
    l_id = lax.broadcasted_iota(jnp.int32, (16, 128), 1)
    k_id = COLS * q + lax.rem(l_id, COLS)
    quad = s_id // 4 + core * (1 - 2 * lax.rem(s_id // 4, 2))
    quad = 2 * lax.rem(quad, 2) + quad // 2

    def masked(s_order):
        i_id = ROWS * r + 16 * (l_id // COLS) + s_order
        return jnp.where((i_id < limit) & (k_id < limit), 1.0, 0.0).astype(F32)

    mask = jnp.stack([masked(4 * quad + lax.rem(s_id, 4)), masked(s_id)])

    planes = sorted(itertools.product(range(4), range(4)), key=lambda d: -(d[0] % 2 + d[1] % 2))

    def send_ab(n, carry):
        ahead = lax.rem(n + 1, 4)
        group = lax.rem(quarter + ahead, 4)
        first = 32 * group
        weights = jnp.concatenate(
            [wt[pl.ds(pl.multiple_of(k * C + first, 32), 32)] for k in range(4)], axis=0
        )

        def gate(piece, inner):
            rhs = zn[pl.ds(4 * piece, 4)].reshape(512, C)
            proj = dot_t(weights, rhs)
            a = sigmoid(proj[0:32]) * proj[32:64]
            b = sigmoid(proj[64:96]) * proj[96:128]
            swapped = 2 * lax.rem(piece, 2) + piece // 2
            place = 4 * (swapped + core * (1 - 2 * lax.rem(swapped, 2)))
            for k in range(4):
                stage[pl.ds(place + k, 32, stride=32)] = a[:, 128 * k : 128 * (k + 1)]
                stage[pl.ds(16 + 4 * piece + k, 32, stride=32)] = b[:, 128 * k : 128 * (k + 1)]
            return inner

        lax.fori_loop(0, 4, gate, 0)
        both = stage[...].reshape(32, 2, 16, 128) * mask
        amsg[pl.ds(first, 32)] = both.astype(BF16)

        @pl.when(n == 0)
        def _():
            pl.semaphore_wait(in_sem, len(peers))


        for dx, dy in planes:
            tx, ty = xs_at[dx], ys_at[dy]
            tz = lax.rem(group + 8 - tx - ty, 4)
            for c in range(2):
                to = device(tx, ty, tz, core_at[c])
                src = amsg.at[first + 8 * tx + 2 * ty + core_at[c]]
                if (dx, dy, c) == (0, 0, 0):
                    post(src, abuf.at[r, q], a_sem.at[0], a_sem.at[1], *to)
                else:
                    push(src, abuf.at[r, q], a_sem.at[0], a_sem.at[1], to)
        return carry

    lax.fori_loop(0, 4, send_ab, 0)

    wait(prow, pair_sem.at[1])

    def tri_gate(s, carry):
        v = prow[s].reshape(HALF, C).astype(F32)
        tg[s] = sigmoid(dot(layer_norm(v).astype(BF16), tri_gate_ref[...]))
        return carry

    lax.fori_loop(0, OWN, tri_gate, 0)

    wait(abuf, a_sem.at[1])
    top = lax.rem(lax.broadcasted_iota(jnp.int32, (1, 16, 128), 1), 8) < 4
    for side in range(2):
        for u in range(4):
            even = abuf[:, 2 * u, side].reshape(256, 128)
            odd = abuf[:, 2 * u + 1, side].reshape(256, 128)
            low = jnp.concatenate([even[:, :64], odd[:, :64]], axis=1)
            high = jnp.concatenate([even[:, 64:], odd[:, 64:]], axis=1)
            if side == 1:
                tiles = [low.reshape(16, 1, 16, 128), high.reshape(16, 1, 16, 128)]
            else:
                tiles = []
                for half in (low, high):
                    half = half.astype(F32).reshape(8, 2, 16, 128)
                    one, two = half[:, 0], half[:, 1]
                    tiles.append(jnp.where(top, one, two).astype(BF16).reshape(8, 1, 16, 128))
                    tiles.append(jnp.where(top, two, one).astype(BF16).reshape(8, 1, 16, 128))
            amat[side, :, 128 * u : 128 * (u + 1)] = jnp.concatenate(tiles, axis=1).reshape(512, 128)

    x = dot_t(amat[0], amat[1]).reshape(8, 8, 8, 512)
    for m in range(8):
        for c in range(2):
            tiles = [x[m, :, :, 128 * t : 128 * (t + 1)] for t in (2 * c, 2 * c + 1)]
            xmsg[2 * m + c] = jnp.concatenate(tiles, axis=1).astype(BF16)

    pltpu.make_async_copy(xmsg.at[r, q], xbuf.at[channel], x_sem.at[1]).start()
    for dx, dy, dz, c in far_first([0, 1]):
        if (dx, dy, dz, c) != (0, 0, 0, 0):
            to = device(xs_at[dx], ys_at[dy], zs_at[dz], core_at[c])
            push(xmsg.at[to[0], to[1]], xbuf.at[channel], x_sem.at[0], x_sem.at[1], to)

    wait(xbuf, x_sem.at[1])
    xs[...] = layer_norm(xbuf[...].astype(F32), 0).reshape(2048, 128)
    row_id = lax.broadcasted_iota(jnp.int32, (16, C), 0)
    columns = jnp.zeros((16, C), F32)
    for h in range(HEADS):
        columns = jnp.where(row_id // 4 == h, abias_ref[h : h + 1, :].astype(F32), columns)
    x_hi = cx // 2

    def spread(block):
        dst = bbuf.at[block, :, core, cz, x_hi, cy]
        for dx, dy, dz, _ in far_first([0]):
            to = device(xs_at[dx], ys_at[dy], zs_at[dz], part)
            if (dx, dy, dz) == (0, 0, 0):
                post(bmsg.at[block], dst, b_send.at[block], b_recv.at[block], *to)
            else:
                push(bmsg.at[block], dst, b_send.at[block], b_recv.at[block], to)

    def spread_done(block):
        @pl.when(core == part)
        def _():
            wait(bbuf.at[block, :, 0], b_send.at[block])
            wait(bbuf.at[block, :, 1, pl.ds(0, 3)], b_send.at[block])
            wait(bbuf.at[block, :, 1, 0, 0, pl.ds(0, 3)], b_send.at[block])
            wait(bbuf.at[block, :, 1, 0, 1], b_send.at[block])

        @pl.when(core != part)
        def _():
            wait(bbuf.at[block], b_send.at[block])

    for block in range(2):
        group = 4 * lax.rem(flip + block, 2)
        bias = jnp.zeros((16, HALF), F32)
        for k in range(4):
            slot = group + k
            normed = []
            for t in range(2):
                xn = xs[pl.ds(8 * t + slot, 128, stride=16)].T.astype(BF16)
                update = dot(xn, tri_out_ref[...])
                v = prow[slot, 2 * t : 2 * t + 2].reshape(128, C).astype(F32)
                first = (v + tg[slot, 128 * t : 128 * (t + 1)] * update).astype(BF16)
                z1[slot, 128 * t : 128 * (t + 1)] = first
                normed.append(layer_norm(first.astype(F32)).astype(BF16))
            normed = jnp.concatenate(normed, axis=0)
            yn[core, slot] = normed
            weights = jnp.where(lax.rem(row_id, 4) == k, columns, 0.0).astype(BF16)
            bias += dot_t(weights, normed)
        for t in range(2):
            bmsg[block, t] = bias[:, 128 * t : 128 * (t + 1)].astype(BF16)
        if block == 0:
            spread(0)
        rows = yn.at[core, pl.ds(group, 4)]
        push(rows, rows, yn_sem.at[0], yn_sem.at[1], (r + 1 - 2 * core, q))

    sub_id = lax.broadcasted_iota(jnp.int32, (128, C), 0)
    upper = lax.rem(sub_id, 8) < 4
    lane_head = lax.broadcasted_iota(jnp.int32, (2, 8, C), 2) // DH
    row_head = 2 * lax.broadcasted_iota(jnp.int32, (2, 8, C), 0) + (
        lax.broadcasted_iota(jnp.int32, (2, 8, C), 1) // 4
    )
    head_mask = jnp.where(lane_head == row_head, 1.0, 0.0).astype(F32)

    def own_qkvg(s, carry):
        qkvg = dot(yn[core, s], qkvg_ref[...])
        query = (qkvg[:, :C] * DH ** (-0.5)).reshape(4, 2, 32, C)
        for block in range(2):
            v = query[:, block].reshape(128, C)
            down, up = pltpu.roll(v, 4, 0), pltpu.roll(v, 124, 0)
            even = jnp.where(upper, v, down).reshape(16, 1, 1, 8, C)
            odd = jnp.where(upper, up, v).reshape(16, 1, 1, 8, C)
            rows = jnp.concatenate([even * head_mask, odd * head_mask], axis=1)
            qx[block, s] = rows.reshape(512, C).astype(BF16)
        kb[core, s] = qkvg[:, C : 2 * C].astype(BF16)
        vb[core, s] = qkvg[:, 2 * C : 3 * C].astype(BF16)
        ag[s] = sigmoid(qkvg[:, 3 * C :])
        return carry

    lax.fori_loop(0, OWN, own_qkvg, 0)
    wait(yn.at[0], yn_sem.at[1])

    def other_kv(s, carry):
        kv = dot(yn[1 - core, s], qkvg_ref[:, C : 3 * C])
        kb[1 - core, s] = kv[:, :C].astype(BF16)
        vb[1 - core, s] = kv[:, C:].astype(BF16)
        return carry

    lax.fori_loop(0, OWN, other_kv, 0)

    def multiply(block):
        def one(s, carry):
            raw[block, s] = dot_t(qx[block, s], kb[:, s].reshape(2 * HALF, C))
            return carry

        lax.fori_loop(0, OWN, one, 0)

    multiply(0)
    spread_done(0)
    spread(1)
    multiply(1)

    key_id = lax.broadcasted_iota(jnp.int32, (1, 2 * HALF), 1)
    key_bias = jnp.where(key_id < limit, 0.0, -1000000000.0).astype(F32)

    def attend(block, s):
        vals = vb[:, s].reshape(2 * HALF, C)
        scores = raw[block, s] + full_bias[...]
        expo = jnp.exp(scores - jnp.max(scores, axis=-1, keepdims=True))
        total = jnp.sum(expo, axis=-1, keepdims=True)
        got = (dot(expo.astype(BF16), vals) / total).reshape(16, 2, 2, 8, C) * head_mask
        got = jnp.sum(got, axis=2)
        even, odd = got[:, 0].reshape(128, C), got[:, 1].reshape(128, C)
        even = even + pltpu.roll(even, 124, 0)
        odd = odd + pltpu.roll(odd, 4, 0)
        return jnp.where(upper, even, odd)

    for block in range(2):
        wait(bbuf.at[block], b_recv.at[block])
        tiles = [bbuf[block, t, c].reshape(512, 128) for c in range(2) for t in range(2)]
        full_bias[...] = jnp.concatenate(tiles, axis=-1).astype(F32) + key_bias

        def finish(s, carry, block=block):
            gate = ag[s].reshape(4, 2, 32, C)[:, block].reshape(128, C)
            first = z1[s].reshape(4, 2, 32, C)[:, block].reshape(128, C)
            gated = (gate * attend(block, s)).astype(BF16)
            done = first.astype(F32) + dot(gated, aout_ref[...])
            omsg[s, :, 32 * block : 32 * (block + 1)] = done.astype(BF16).reshape(4, 32, C)
            side = lax.rem(s // 4 + flip, 2)
            for u in range(4):
                src = omsg.at[s, u, pl.ds(32 * block, 32)]
                dst = out_ref.at[4 * q + lax.rem(s, 4), pl.ds(32 * block, 32)]
                post(src, dst, o_sem.at[0], o_sem.at[1], 2 * (r // 2) + side, 4 * core + u)
            return carry

        lax.fori_loop(0, OWN, finish, 0)

    wait(amsg.at[pl.ds(0, N_DEV - 1)], a_sem.at[0])
    wait(xbuf.at[pl.ds(0, N_DEV - 1)], x_sem.at[0])
    own_block = core == q // 4
    @pl.when(own_block)
    def _():
        wait(prow.at[pl.ds(0, 7)], pair_sem.at[0])
        wait(prow.at[pl.ds(0, 7)], o_sem.at[0])

    @pl.when(jnp.logical_not(own_block))
    def _():
        wait(prow, pair_sem.at[0])
        wait(prow, o_sem.at[0])

    wait(yn.at[0], yn_sem.at[0])
    spread_done(1)
    wait(out_ref, o_sem.at[1])


def local(pair, valid_len, tri_in, tri_gate, tri_out, att_qkvg, att_bias, att_out):
    hbm = pl.BlockSpec(memory_space=pl.ANY)

    def hold(array):
        return pltpu.with_memory_space_constraint(array, pltpu.HBM)

    smem = pl.BlockSpec(memory_space=pltpu.SMEM)
    dma = pltpu.SemaphoreType.DMA
    return pl.pallas_call(
        kernel,
        out_shape=jax.ShapeDtypeStruct(pair.shape, pair.dtype),
        in_specs=[hbm, smem] + [hbm] * 6,
        out_specs=hbm,
        scratch_shapes=[
            pltpu.VMEM(tri_in.shape, BF16),
            pltpu.VMEM(tri_gate.shape, BF16),
            pltpu.VMEM(tri_out.shape, BF16),
            pltpu.VMEM(att_qkvg.shape, BF16),
            pltpu.VMEM(att_bias.shape[::-1], BF16),
            pltpu.VMEM(att_out.shape, BF16),
            pltpu.VMEM((ROWS, COLS, C), BF16),
            pltpu.VMEM((16, 2, COLS, C), BF16),
            pltpu.VMEM((4 * C, C), BF16),
            pltpu.VMEM((1024, 128), F32),
            pltpu.VMEM((N_DEV, 2, 16, 128), BF16),
            pltpu.VMEM((N_ROW, N_COL, 2, 16, 128), BF16),
            pltpu.VMEM((2, 512, 512), BF16),
            pltpu.VMEM((N_ROW, N_COL, 16, 128), BF16),
            pltpu.VMEM((N_DEV, 16, 128), BF16),
            pltpu.VMEM((2048, 128), F32),
            pltpu.VMEM((OWN, 4, COLS, C), BF16),
            pltpu.VMEM((OWN, HALF, C), F32),
            pltpu.VMEM((OWN, HALF, C), BF16),
            pltpu.VMEM((2, OWN, HALF, C), BF16),
            pltpu.VMEM((2, 2, 16, 128), BF16),
            pltpu.VMEM((2, 2, 2, 4, 2, 4, 16, 128), BF16),
            pltpu.VMEM((2, OWN, 512, C), BF16),
            pltpu.VMEM((2, OWN, HALF, C), BF16),
            pltpu.VMEM((2, OWN, HALF, C), BF16),
            pltpu.VMEM((OWN, HALF, C), F32),
            pltpu.VMEM((OWN, 4, COLS, C), BF16),
            pltpu.VMEM((512, 2 * HALF), F32),
            pltpu.VMEM((2, OWN, 512, 2 * HALF), F32),
            dma((7,)),
            pltpu.SemaphoreType.REGULAR,
            dma((2,)),
            dma((2,)),
            dma((2,)),
            dma((2,)),
            dma((2,)),
            dma((2,)),
            dma((2,)),
        ],
        compiler_params=pltpu.CompilerParams(
            collective_id=0, has_side_effects=True, vmem_limit_bytes=52 * 2**20
        ),
        name="pairformer",
    )(hold(pair), valid_len, hold(tri_in), hold(tri_gate), hold(tri_out), hold(att_qkvg), hold(att_bias.T), hold(att_out))


def solution(mesh):
    placed = (P("row", "col", None), P(), P(), P(), P(), P(), P(), P())
    return jax.shard_map(
        local, mesh=mesh, in_specs=placed, out_specs=P("row", "col", None), check_vma=False
    )
```
